32 devices in a mesh: dp: 8 (over z, x), tensor: 4 (over y, core).
Axes of the slice: x: 2, y: 2, z: 4, core: 2. Of those that a mesh axis runs over, the one named last changes fastest.
Arguments:
- tokens: bfloat16 [16384, 1024], P('dp'), may hold values from -6 to 6
- segment_ids: int32 [16, 1024], P('dp'), may hold values from 0 to 7, never falling along the last dimension, each value on 1 to 512 neighbouring positions
- ln_gain: float32 [1024], replicated, may hold values from 0.1 to 1.9
- ln_bias: float32 [1024], replicated, may hold values from -1.75 to 1.75
- qkv_weight: bfloat16 [1024, 3, 1024], P(None, None, 'tensor'), may hold values from -0.1875 to 0.1875
- qkv_bias: float32 [3, 1024], P(None, 'tensor'), may hold values from -3 to 3
- dense_weight: bfloat16 [1024, 1024], P('tensor'), may hold values from -0.75 to 0.75
- dense_bias: float32 [1024], replicated, may hold values from -1.75 to 1.75
- fc1_weight: bfloat16 [1024, 4096], P(None, 'tensor'), may hold values from -0.1875 to 0.1875
- fc1_bias: float32 [4096], P('tensor'), may hold values from -3 to 3
- fc2_weight: bfloat16 [4096, 1024], P('tensor'), may hold values from -0.09375 to 0.09375
- fc2_bias: float32 [1024], replicated, may hold values from -1.75 to 1.75
- cotangent: bfloat16 [16384, 1024], P('dp'), may hold values from -6 to 6
Outputs:
- mixed: bfloat16 [16384, 1024], P('dp')
- input_grad: bfloat16 [16384, 1024], P('dp')
- ln_gain_grad: float32 [1024], replicated
- ln_bias_grad: float32 [1024], replicated
- qkv_weight_grad: float32 [1024, 3, 1024], P(None, None, 'tensor')
- qkv_bias_grad: float32 [3, 1024], P(None, 'tensor')
- dense_weight_grad: float32 [1024, 1024], P('tensor')
- dense_bias_grad: float32 [1024], replicated
- fc1_weight_grad: float32 [1024, 4096], P(None, 'tensor')
- fc1_bias_grad: float32 [4096], P('tensor')
- fc2_weight_grad: float32 [4096, 1024], P('tensor')
- fc2_bias_grad: float32 [1024], replicated
The draws below stay inside these ranges and needn't reach their ends.
Inputs may be any that keep to these rules, and one draw needn't show every extreme that they name: `segment_ids`: along each sequence the ids never fall; each of the 8 documents of a sequence holds at least one token and at most half of the 1024 tokens, and one holds exactly half.
All inputs are finite; a program needn't handle non-finite values.
Results may differ from the reference program's by a relative error of at most 0.014.
Values may be sent and summed in bfloat16 or wider, within the bound.
A program may use at most 192 MiB of HBM per device.

```python
import math
import jax
import jax.numpy as jnp
import numpy as np
from jax import lax

D = 1024
HEADS = 16
HEAD = 64
ROTARY = 32
FF = 4096
SEQ = 1024
DOCS = 8
SEQS_DEV = 2
SEQS = 16
TOKENS = 16384
N_DP = 8


def shard_levels(stream_key, dims, cuts, low, high):
    def one(axis_at, shards_of):
        draws = jax.random.uniform(jax.random.fold_in(jax.random.fold_in(stream_key, 6), axis_at), (shards_of,), jnp.float32, low / len(cuts), high / len(cuts))
        return jnp.repeat(jnp.exp(draws), dims[axis_at] // shards_of).reshape((-1,) + (1,) * (len(dims) - axis_at - 1))

    gain = one(*cuts[0])
    for cut in cuts[1:]:
        gain = gain * one(*cut)
    return gain


def length_profile(number_of, total, reach, lean):
    weights = [(1 << 20) // math.isqrt(standing ** lean) + 1 for standing in range(2, number_of + 1)]
    spare, counts = total - reach - (number_of - 1), [1] * (number_of - 1)
    while spare > 0:
        candidates = [i for i in range(number_of - 1) if counts[i] < reach]
        pool, budget = sum([weights[i] for i in candidates]), spare
        for i in candidates:
            addition = min(reach - counts[i], max(1, budget * weights[i] // pool), spare)
            counts[i] = counts[i] + addition
            spare = spare - addition
    return np.array([reach] + counts)


def uneven(key, amount, total, reach, lean):
    if amount == 2:
        one = jax.random.randint(key, (), max(1, total - reach), min(reach, total - 1) + 1)
        return jnp.stack([one, total - one])
    sizes = jnp.asarray(length_profile(amount, total, reach, lean), jnp.int32)
    pairs = (amount - 1) // 2
    donor, receiver = sizes[1:1 + 2 * pairs:2], sizes[2:2 + 2 * pairs:2]
    room = jnp.minimum(donor - 1, reach - receiver)
    shifted = jax.random.randint(jax.random.fold_in(key, 1), (pairs,), 0, 1 << 20) % (room + 1)
    sizes = sizes.at[1:1 + 2 * pairs:2].set(donor - shifted).at[2:2 + 2 * pairs:2].set(receiver + shifted)
    return sizes[jax.random.permutation(jax.random.fold_in(key, 2), amount)]


def normal_values(rng, dims, scale, limit, cuts=(), held_as=jnp.bfloat16):
    drawn = scale * jax.random.normal(rng, dims, jnp.float32)
    if cuts:
        drawn = drawn * shard_levels(rng, dims, cuts, -0.22, 0.18)
    return jnp.clip(drawn, -limit, limit).astype(held_as)


def setup_inputs(seed: int = 0) -> dict:
    key_of = jax.random.split(jax.random.key(seed), 14)
    tokens = normal_values(key_of[0], (TOKENS, D), 1.0, 6.0, ((0, 8),))
    segment_ids = jax.vmap(lambda own: jnp.searchsorted(jnp.cumsum(uneven(own, DOCS, SEQ, SEQ // 2, 0)), jnp.arange(SEQ), side="right"))(jax.random.split(key_of[1], SEQS)).reshape((SEQS, SEQ)).astype(jnp.int32)
    ln_gain = jnp.clip(1.0 + 0.18 * jax.random.normal(key_of[2], (D,), jnp.float32), 0.1, 1.9)
    ln_bias = normal_values(key_of[3], (D,), 0.3, 1.75, (), jnp.float32)
    qkv_weight = normal_values(key_of[4], (D, 3, D), D ** -0.5, 0.1875, ((2, 4),))
    qkv_bias = normal_values(key_of[5], (3, D), 0.5, 3.0, ((1, 4),), jnp.float32)
    dense_weight = normal_values(key_of[6], (D, D), (D // 16) ** -0.5, 0.75, ((0, 4),))
    dense_bias = normal_values(key_of[7], (D,), 0.3, 1.75, (), jnp.float32)
    fc1_weight = normal_values(key_of[8], (D, FF), D ** -0.5, 0.1875, ((1, 4),))
    fc1_bias = normal_values(key_of[9], (FF,), 0.5, 3.0, ((0, 4),), jnp.float32)
    fc2_weight = normal_values(key_of[10], (FF, D), FF ** -0.5, 0.09375, ((0, 4),))
    fc2_bias = normal_values(key_of[11], (D,), 0.3, 1.75, (), jnp.float32)
    cotangent = normal_values(key_of[12], (TOKENS, D), 1.0, 6.0, ((0, 8),))
    return dict(tokens=tokens, segment_ids=segment_ids, ln_gain=ln_gain, ln_bias=ln_bias, qkv_weight=qkv_weight, qkv_bias=qkv_bias, dense_weight=dense_weight, dense_bias=dense_bias, fc1_weight=fc1_weight, fc1_bias=fc1_bias, fc2_weight=fc2_weight, fc2_bias=fc2_bias, cotangent=cotangent)


highest = lax.Precision.HIGHEST
norm_eps = 1e-05
masked_score = -1e+30
rotary_base = 10000.0

@jax.custom_vjp
def low(v):
    return lax.optimization_barrier(v.astype(jnp.bfloat16)).astype(jnp.float32)

@jax.custom_vjp
def low_back(v):
    return v

def low_keep(v):
    return (low(v), None)

def low_pass(kept, grad):
    return (grad,)

def back_keep(v):
    return (v, None)

def back_low(kept, grad):
    return (low(grad),)
low.defvjp(low_keep, low_pass)
low_back.defvjp(back_keep, back_low)

def product(left_side, right_side):
    return jnp.dot(left_side, right_side, precision=highest, preferred_element_type=jnp.float32)

def rotary_tables(length, rotary_dims):
    half_dims = rotary_dims // 2
    frequency = rotary_base ** (-(jnp.arange(half_dims, dtype=jnp.float32) * 2.0) / rotary_dims)
    angles = jnp.arange(length, dtype=jnp.float32)[:, None] * frequency[None, :]
    return (jnp.cos(angles)[:, None, :], jnp.sin(angles)[:, None, :])

def rotate(head_field, cosine_table, sine_table, rotary_dims):
    half_dims = rotary_dims // 2
    first_half = head_field[..., :half_dims]
    second_half = head_field[..., half_dims:rotary_dims]
    return jnp.concatenate([first_half * cosine_table - second_half * sine_table, second_half * cosine_table + first_half * sine_table, head_field[..., rotary_dims:]], axis=-1)

def attend_sequence(pieces):
    query_rot, key_rot, value_low, segment_row = pieces
    seq_length = segment_row.shape[0]
    score_scale = query_rot.shape[-1] ** (-0.5)
    places = jnp.arange(seq_length, dtype=jnp.int32)
    allowed = (places[None, :] <= places[:, None]) & (segment_row[None, :] == segment_row[:, None])
    scores = jnp.einsum('qhd,khd->hqk', query_rot, key_rot, precision=highest) * score_scale
    scores = low_back(scores)
    scores = jnp.where(allowed[None], scores, masked_score)
    row_peak = lax.optimization_barrier(jnp.max(scores, axis=-1, keepdims=True))
    weights = jnp.exp(scores - row_peak)
    weights_low = low(weights / lax.optimization_barrier(jnp.sum(weights, axis=-1, keepdims=True)))
    return jnp.einsum('hqk,khd->qhd', weights_low, value_low, precision=highest)

def phi_layer(rows_in, segments, parameters):
    ln_gain, ln_bias, qkv_weight, qkv_bias, dense_weight, dense_bias, fc1_weight, fc1_bias, fc2_weight, fc2_bias = parameters
    seq_count, seq_length = segments.shape
    row_mean = lax.optimization_barrier(jnp.mean(rows_in, axis=-1, keepdims=True))
    centred = rows_in - row_mean
    variance = lax.optimization_barrier(jnp.mean(centred * centred, axis=-1, keepdims=True))
    normed = low(centred * lax.rsqrt(variance + norm_eps) * ln_gain + ln_bias)
    packed = product(normed, qkv_weight.reshape(D, 3 * D)) + qkv_bias.reshape(3 * D)
    packed = low_back(packed).reshape(seq_count, seq_length, 3, HEADS, HEAD)
    cosine_table, sine_table = rotary_tables(seq_length, ROTARY)
    query_rot = low(rotate(packed[:, :, 0], cosine_table, sine_table, ROTARY))
    key_rot = low(rotate(packed[:, :, 1], cosine_table, sine_table, ROTARY))
    value_low = low(packed[:, :, 2])
    context = lax.map(jax.checkpoint(attend_sequence), (query_rot, key_rot, value_low, segments))
    context = low(low_back(context.reshape(seq_count * seq_length, D)))
    hidden = low_back(product(normed, fc1_weight) + fc1_bias)
    active = low(jax.nn.gelu(hidden, approximate=True))
    return rows_in + product(context, dense_weight) + product(active, fc2_weight) + dense_bias + fc2_bias

def reference(tokens, segment_ids, ln_gain, ln_bias, qkv_weight, qkv_bias, dense_weight, dense_bias, fc1_weight, fc1_bias, fc2_weight, fc2_bias, cotangent):
    parameters = (ln_gain.astype(jnp.float32), ln_bias.astype(jnp.float32), qkv_weight.astype(jnp.float32), qkv_bias.astype(jnp.float32), dense_weight.astype(jnp.float32), dense_bias.astype(jnp.float32), fc1_weight.astype(jnp.float32), fc1_bias.astype(jnp.float32), fc2_weight.astype(jnp.float32), fc2_bias.astype(jnp.float32))
    group_rows = SEQS_DEV * SEQ
    token_groups = tokens.astype(jnp.float32).reshape(N_DP, group_rows, D)
    cotangent_groups = cotangent.astype(jnp.float32).reshape(N_DP, group_rows, D)
    segment_groups = segment_ids.reshape(N_DP, SEQS_DEV, SEQ)

    def one_group(running, pieces):
        rows_in, rows_back, segments = pieces

        def forward(rows_value, weights_all):
            return phi_layer(rows_value, segments, weights_all)
        result, pullback = jax.vjp(forward, rows_in, parameters)
        rows_grad, weight_grads = pullback(rows_back)
        running = jax.tree.map(lambda total_part, new_part: total_part + new_part, running, weight_grads)
        return (running, (result, rows_grad))
    zero_grads = jax.tree.map(jnp.zeros_like, parameters)
    summed, (results, row_grads) = lax.scan(one_group, zero_grads, (token_groups, cotangent_groups, segment_groups))
    return (results.reshape(TOKENS, D).astype(jnp.bfloat16), row_grads.reshape(TOKENS, D).astype(jnp.bfloat16), summed[0], summed[1], summed[2], summed[3], summed[4], summed[5], summed[6], summed[7], summed[8], summed[9])
```

```python
import functools
import heapq

import jax
import jax.numpy as jnp
import numpy as np
from jax import lax
from jax.experimental import pallas as pl
from jax.experimental.pallas import tpu as pltpu
from jax.sharding import PartitionSpec as P

HEAD = 64
ROTARY = 32
NORM_EPS = 1e-05
MASKED = -1e30
BASE = 10000.0
BF = jnp.bfloat16
F32 = jnp.float32
MESH = pl.DeviceIdType.MESH
GROUP = 8


def dot(a, b):
    return lax.dot_general(a, b, (((1,), (0,)), ((), ())), preferred_element_type=F32)


def dot_nt(a, b):
    return lax.dot_general(a, b, (((1,), (1,)), ((), ())), preferred_element_type=F32)


def dot_tn(a, b):
    return lax.dot_general(a, b, (((0,), (0,)), ((), ())), preferred_element_type=F32)


def rotary_tables(length):
    half = ROTARY // 2
    frequency = (BASE ** (-(np.arange(half, dtype=np.float32) * 2.0) / ROTARY)).astype(np.float32)
    angles = np.arange(length, dtype=np.float32)[:, None] * frequency[None, :]
    cosine, sine = np.cos(angles), np.sin(angles)
    rest = HEAD - ROTARY
    c = np.concatenate([cosine, cosine, np.ones((length, rest), np.float32)], axis=1)
    s = np.concatenate([-sine, sine, np.zeros((length, rest), np.float32)], axis=1)
    return np.tile(c, (1, 2)).astype(np.float32), np.tile(s, (1, 2)).astype(np.float32)


def pair_swap(u):
    lane = lax.broadcasted_iota(jnp.int32, u.shape, 1)
    half = ROTARY // 2
    return jnp.where(lane % ROTARY < half, pltpu.roll(u, 128 - half, 1), pltpu.roll(u, half, 1))


class Clock:
    def __init__(self):
        self.now = 0.0
        self.queue = []
        self.count = 0
        self.free = {}

    def at(self, when, step):
        heapq.heappush(self.queue, (when, self.count, step))
        self.count += 1

    def arrival(self, link, mib, rate):
        start = max(self.now, self.free.get(link, 0.0))
        self.free[link] = start + mib * rate
        return self.free[link] + 2.0

    def run(self, cost, work):
        while self.queue and self.queue[0][0] <= self.now:
            heapq.heappop(self.queue)[2]()
        work()
        self.now += cost

    def advance(self):
        when, _, step = heapq.heappop(self.queue)
        self.now = max(self.now, when)
        step()

    def drain(self):
        while self.queue:
            self.advance()


LINK_US = 22.5
CORE_US = 2.0


def layer_kernel(
    x_hbm, g_hbm, wqkv_hbm, wd_hbm, w1_hbm, w2_hbm,
    seg_ref, gain_ref, lnb_ref, bqkv_ref, db_ref, b1_ref, b2_ref, cos_ref, sin_ref,
    mixed_hbm, igrad_hbm, fc2_hbm, fc1_hbm, qkv_hbm, dense_hbm, norm_out,
    nb, gb, act, dh, wqkv, wd, w1, w2,
    qs, kmask, vmask, qT, cg, cgT, ctx, pg, dkT, dvT, bias, gacc, bacc,
    pt, t1r, t2r, xs, gA, gQ, gD, xrA, ziA, zmA, xrQ, ziQ, zmQ, xrD, ziD, zmD,
    small_send, small_core, small_recv,
    load_sem, x_sem, dp_send, dp_recv, t_send, t_recv, sm_send, sm_recv, credit,
):
    rows, width = nb.shape
    seqs, length = seg_ref.shape
    local = wd.shape[0]
    ff = w1.shape[1]
    heads = local // HEAD
    QB = 256
    nrb = rows // QB
    HB = QB // 2

    dp, tensor = lax.axis_index("dp"), lax.axis_index("tensor")
    base = dp - lax.rem(dp, GROUP)
    me = lax.rem(dp, GROUP)
    xx, zz = lax.rem(me, 2), me // 2
    yy, cc = tensor // 2, lax.rem(tensor, 2)
    x_dev = (base + zz * 2 + (1 - xx), tensor)
    pair_dev = (base + (zz + 1 - 2 * lax.rem(zz, 2)) * 2 + xx, tensor)
    mid_dev = (base + (3 - zz) * 2 + xx, tensor)
    y_dev = (dp, (1 - yy) * 2 + cc)
    c_dev = (dp, yy * 2 + (1 - cc))
    inner = (zz == 1) | (zz == 2)
    outer = jnp.logical_not(inner)
    dp_devs = [(base + lax.rem(me + k, GROUP), tensor) for k in range(1, GROUP)]

    barrier = pltpu.get_barrier_semaphore()
    for device in dp_devs + [y_dev, c_dev]:
        pl.semaphore_signal(barrier, inc=1, device_id=device, device_id_type=MESH)

    loads = {}

    def load(name, k, src, dst):
        loads[name] = pltpu.make_async_copy(src, dst, load_sem.at[k])
        loads[name].start()

    quarter = rows // 4
    for k in range(4):
        part = pl.ds(k * quarter, quarter)
        load(f"x{k}", k, x_hbm.at[part], act.at[part])
    load("w1", 4, w1_hbm, w1)
    load("g", 5, g_hbm, gb)
    load("w2", 6, w2_hbm, w2)
    load("wqkv", 7, wqkv_hbm, wqkv)
    load("wd", 8, wd_hbm, wd)

    clock = Clock()
    sends = []

    def remote(src, dst, send_sem, recv_sem, device):
        copy = pltpu.make_async_remote_copy(
            src_ref=src, dst_ref=dst, send_sem=send_sem, recv_sem=recv_sem,
            device_id=device, device_id_type=MESH,
        )
        return copy

    def add_into(dst, a_ref, b_ref, n):
        step = 48 if n % 48 == 0 else 32

        @pl.loop(0, n // step)
        def _(k):
            r = pl.ds(pl.multiple_of(k * step, 16), step)
            dst[r, :] = (a_ref[r, :].astype(F32) + b_ref[r, :].astype(F32)).astype(BF)

    class Chunk:
        def __init__(self, number, own, xr, zi, zm, out, out_row):
            self.number, self.own, self.xr, self.zi, self.zm = number, own, xr, zi, zm
            self.out, self.out_row = out, out_row
            n, cols = own.shape
            self.half = n // 2
            self.mib = self.half * cols * 2 / 2**20
            h = self.half
            keep = pl.ds(pl.multiple_of(xx * h, 16), h)
            give = pl.ds(pl.multiple_of((1 - xx) * h, 16), h)
            self.keep = own.at[keep]
            self.target = out.at[pl.ds(pl.multiple_of(out_row + xx * h, 16), h)]
            k = number
            self.c_x = remote(own.at[give], xr, dp_send.at[k, 0], dp_recv.at[k, 0], x_dev)
            self.c_in = remote(xr, zi, dp_send.at[k, 1], dp_recv.at[k, 1], pair_dev)
            self.c_mid = remote(zi, zm, dp_send.at[k, 2], dp_recv.at[k, 2], mid_dev)
            self.c_out = remote(zm, zm, dp_send.at[k, 1], dp_recv.at[k, 2], pair_dev)
            self.c_ag = remote(zm, self.target, dp_send.at[k, 3], dp_recv.at[k, 3], x_dev)
            self.c_loc = pltpu.make_async_copy(zm, self.target, dp_send.at[k, 4])

        def start(self):
            self.c_x.start()
            clock.at(clock.arrival("x", self.mib, LINK_US), self.pair_sum)

        def pair_sum(self):
            self.c_x.wait_recv()
            add_into(self.xr, self.xr, self.keep, self.half)

            @pl.when(outer)
            def _():
                self.c_in.start()

            clock.at(clock.arrival("zin", self.mib, LINK_US), self.side_sum)

        def side_sum(self):
            @pl.when(inner)
            def _():
                self.c_in.wait_recv()
                add_into(self.zi, self.zi, self.xr, self.half)
                self.c_mid.start()

            clock.at(clock.arrival("zmid", self.mib, LINK_US), self.line_sum)

        def line_sum(self):
            @pl.when(inner)
            def _():
                self.c_mid.wait_recv()
                self.c_mid.wait_send()
                add_into(self.zm, self.zm, self.zi, self.half)
                self.c_out.start()
                self.c_ag.start()
                self.c_loc.start()

            clock.arrival("x", self.mib, LINK_US)
            clock.at(clock.arrival("zout", self.mib, LINK_US), self.outer_end)

        def outer_end(self):
            @pl.when(outer)
            def _():
                self.c_mid.wait_recv()
                self.c_ag.start()
                self.c_loc.start()

        def finish(self):
            self.c_x.wait_send()
            self.c_in.wait_send()
            self.c_ag.wait()
            self.c_loc.wait()

    chunks = []

    def new_chunk(own, xr, zi, zm, out, out_row):
        chunk = Chunk(len(chunks), own, xr, zi, zm, out, out_row)
        chunks.append(chunk)
        chunk.start()

    y_order = []
    mine = pl.ds(pl.multiple_of(cc * HB, 16), HB)
    other = pl.ds(pl.multiple_of((1 - cc) * HB, 16), HB)

    def fetch(seq):
        if seq < len(y_order):
            rb = y_order[seq][1]
            src = x_hbm.at[pl.ds(pl.multiple_of(rb * QB + cc * HB, 16), HB)]
            pltpu.make_async_copy(src, xs.at[seq % 2], x_sem.at[seq % 2]).start()

    def row_stats(x):
        mu = jnp.mean(x, axis=1, keepdims=True)
        cent = x - mu
        rstd = lax.rsqrt(jnp.mean(cent * cent, axis=1, keepdims=True) + NORM_EPS)
        return cent * rstd, rstd

    class RowSum:
        def __init__(self, phase, rb):
            self.phase, self.rb, self.done = phase, rb, False
            k = phase * nrb + rb
            self.k = k
            out = igrad_hbm if phase else mixed_hbm
            self.target = out.at[pl.ds(pl.multiple_of(rb * QB + cc * HB, 16), HB)]
            own = pt.at[rb, mine]
            self.own = own
            self.c_core = remote(pt.at[rb, other], t1r.at[rb], t_send.at[k, 0], t_recv.at[k, 0], c_dev)
            self.c_y = remote(own, t2r.at[rb], t_send.at[k, 1], t_recv.at[k, 1], y_dev)
            self.c_fin = remote(t2r.at[rb], self.target, t_send.at[k, 2], t_recv.at[k, 2], c_dev)
            self.c_loc = pltpu.make_async_copy(t2r.at[rb], self.target, t_send.at[k, 3])

        def start(self):
            if self.phase:
                before = row_sums[(0, self.rb)]
                before.c_fin.wait_recv()
            self.c_core.start()
            clock.at(clock.arrival("c", HB * width * 2 / 2**20, CORE_US), self.chip_sum)

        def chip_sum(self):
            self.c_core.wait_recv()
            add_into(self.own, self.own, t1r.at[self.rb], HB)
            if self.phase:
                pl.semaphore_wait(credit.at[self.rb], 1)
            self.c_y.start()
            clock.at(clock.arrival("y", HB * width * 2 / 2**20, LINK_US), self.whole_sum)

        def whole_sum(self):
            rb = self.rb
            seq = y_order.index((self.phase, rb))
            slot = seq % 2
            fetch(seq + 1)
            pltpu.make_async_copy(x_hbm.at[pl.ds(0, HB)], xs.at[slot], x_sem.at[slot]).wait()
            self.c_y.wait_recv()
            step = 32
            own, arrived = self.own, t2r.at[rb]

            @pl.loop(0, HB // step)
            def _(k):
                r = pl.ds(pl.multiple_of(k * step, 16), step)
                x = xs[slot, r, :].astype(F32)
                total = own[r, :].astype(F32) + arrived[r, :].astype(F32)
                if self.phase == 0:
                    arrived[r, :] = (x + total + (db_ref[...] + b2_ref[...])).astype(BF)
                else:
                    xhat, rstd = row_stats(x)
                    gacc[0:8, :] += jnp.sum((total * xhat).reshape(step // 8, 8, width), axis=0)
                    gacc[8:16, :] += jnp.sum(total.reshape(step // 8, 8, width), axis=0)
                    e = total * gain_ref[...]
                    m1 = jnp.mean(e, axis=1, keepdims=True)
                    m2 = jnp.mean(e * xhat, axis=1, keepdims=True)
                    gr = pl.ds(pl.multiple_of(rb * QB + cc * HB + k * step, 16), step)
                    grad = gb[gr, :].astype(F32) + rstd * (e - m1 - xhat * m2)
                    arrived[r, :] = grad.astype(BF)

            self.c_fin.start()
            self.c_loc.start()
            if self.phase == 0:
                clock.at(clock.now + 4.0, self.give_back)
            elif seq == len(y_order) - 1:
                clock.at(clock.now, norm_sums)

        def give_back(self):
            self.c_fin.wait_send()
            self.c_loc.wait()
            self.c_core.wait_send()
            self.c_y.wait_send()
            pl.semaphore_signal(credit.at[self.rb], inc=1, device_id=y_dev, device_id_type=MESH)
            self.done = True

        def finish(self):
            if self.phase:
                self.c_core.wait_send()
                self.c_y.wait_send()
                self.c_fin.wait()
                self.c_loc.wait()

    row_sums = {}

    def new_rows(phase, rb):
        row_sums[(phase, rb)] = RowSum(phase, rb)
        row_sums[(phase, rb)].start()

    small = {}

    def norm_sums():
        quarter_w = width // 4
        for kind in range(2):
            line = jnp.sum(gacc[kind * 8:kind * 8 + 8, :], axis=0, keepdims=True)
            for k in range(4):
                small_send[kind * 4 + k:kind * 4 + k + 1, :] = line[:, k * quarter_w:(k + 1) * quarter_w]
        swap = remote(small_send, small_core, sm_send.at[0], sm_recv.at[0], c_dev)
        swap.start()
        swap.wait()
        small_send[...] = small_send[...] + small_core[...]
        copies = []
        for k, device in enumerate(dp_devs):
            copy = remote(small_send, small_recv.at[k], sm_send.at[k + 1], sm_recv.at[k + 1], device)
            copy.start()
            copies.append(copy)
        small["copies"] = copies

    def norm_finish():
        for copy in small["copies"]:
            copy.wait()
        total = jnp.zeros(small_send.shape, F32)
        for place in range(GROUP):
            behind = lax.rem(me - place + GROUP, GROUP)
            slot = jnp.maximum(behind - 1, 0)
            there = small_recv[slot]
            total = total + jnp.where(behind == 0, small_send[...], there)
        norm_out[...] = total

    def wait_load(*names):
        for name in names:
            if name in loads:
                loads.pop(name).wait()

    def norm_forward():
        for k in range(4):
            wait_load(f"x{k}")
            step = 64

            @pl.loop(k * quarter // step, (k + 1) * quarter // step)
            def _(i):
                r = pl.ds(pl.multiple_of(i * step, 16), step)
                xhat, _ = row_stats(act[r, :].astype(F32))
                nb[r, :] = (xhat * gain_ref[...] + lnb_ref[...]).astype(BF)

    def cotangent_sum():
        wait_load("g")
        step = 64
        bacc[...] = jnp.zeros_like(bacc)
        gacc[...] = jnp.zeros_like(gacc)

        @pl.loop(0, rows // step)
        def _(i):
            r = pl.ds(pl.multiple_of(i * step, 16), step)
            bacc[16:24, :] += jnp.sum(gb[r, :].astype(F32).reshape(step // 8, 8, width), axis=0)

    def feed_forward(j, first, count):
        wait_load("w1", "g", "w2")
        step = 512
        cols = slice(j * 256, (j + 1) * 256)
        k0 = 0.7978845608028654

        @pl.loop(first // step, (first + count) // step)
        def _(i):
            r = pl.ds(pl.multiple_of(i * step, 16), step)
            h = dot(nb[r, :], w1[:, cols]) + b1_ref[:, cols]
            up = dot_nt(gb[r, :], w2[cols, :])
            h2 = h * h
            th = jnp.tanh(k0 * h * (1.0 + 0.044715 * h2))
            half = 0.5 * (1.0 + th)
            act[r, cols] = (h * half).astype(BF)
            slope = half + 0.5 * h * (1.0 - th * th) * (k0 * (1.0 + 3 * 0.044715 * h2))
            hg = (up * slope).astype(BF)
            dh[r, cols] = hg
            bacc[0:8, cols] += jnp.sum(hg.astype(F32).reshape(step // 8, 8, 256), axis=0)

    def fc2_chunk(j):
        gA[j] = dot_tn(act[:, j * 256:(j + 1) * 256], gb[...]).astype(BF)
        new_chunk(gA.at[j], xrA.at[j], ziA.at[j], zmA.at[j], fc2_hbm, j * 256)

    nf = ff // 256

    def fc1_chunk(j):
        gA[nf + j] = dot_tn(nb[:, j * 256:(j + 1) * 256], dh[...]).astype(BF)
        k = nf + j
        new_chunk(gA.at[k], xrA.at[k], ziA.at[k], zmA.at[k], fc1_hbm, j * 256)

    def qkv_chunk(j):
        gQ[j] = dot_tn(nb[:, j * 256:(j + 1) * 256], pg[...]).astype(BF)
        new_chunk(gQ.at[j], xrQ.at[j], ziQ.at[j], zmQ.at[j], qkv_hbm, j * 256)

    def dense_chunk():
        gD[0:local, :] = dot_tn(ctx[...], gb[...]).astype(BF)
        lines = [jnp.sum(bacc[8 * k:8 * k + 8, :], axis=0, keepdims=True) for k in range(3)]
        pad = jnp.zeros((gD.shape[0] - local - 3, width), F32)
        gD[local:, :] = jnp.concatenate(lines + [pad], axis=0).astype(BF)
        new_chunk(gD, xrD, ziD, zmD, dense_hbm, 0)

    def project(s):
        wait_load("wqkv")

        @pl.loop(0, length // 256)
        def _(i):
            r = pl.ds(pl.multiple_of(i * 256, 256), 256)
            src = pl.ds(pl.multiple_of(s * length + i * 256, 256), 256)
            y = dot(nb[src, :], wqkv[...]) + bqkv_ref[...]
            c, sn = cos_ref[r, :], sin_ref[r, :]
            low = lax.broadcasted_iota(jnp.int32, (256, 128), 1) < HEAD
            for pr in range(heads // 2):
                u = y[:, pr * 128:(pr + 1) * 128]
                u = (u * c + pair_swap(u) * sn) * (HEAD ** -0.5)
                qs[r, pr * 128:(pr + 1) * 128] = u.astype(BF)
                qT[pr * 128:(pr + 1) * 128, r] = u.T.astype(BF)
                u = y[:, local + pr * 128:local + (pr + 1) * 128]
                u = u * c + pair_swap(u) * sn
                kmask[2 * pr, r, :] = jnp.where(low, u, 0.0).astype(BF)
                kmask[2 * pr + 1, r, :] = jnp.where(low, 0.0, u).astype(BF)
                u = y[:, 2 * local + pr * 128:2 * local + (pr + 1) * 128]
                vmask[2 * pr, r, :] = jnp.where(low, u, 0.0).astype(BF)
                vmask[2 * pr + 1, r, :] = jnp.where(low, 0.0, u).astype(BF)

    def context_grad(s):
        wait_load("wd")
        dkT[...] = jnp.zeros_like(dkT)
        dvT[...] = jnp.zeros_like(dvT)

        @pl.loop(0, length // 256)
        def _(i):
            r = pl.ds(pl.multiple_of(i * 256, 256), 256)
            src = pl.ds(pl.multiple_of(s * length + i * 256, 256), 256)
            u = dot_nt(gb[src, :], wd[...])
            cg[r, :] = u.astype(BF)
            cgT[:, r] = u.T.astype(BF)

    def attend(s, i):
        blocks = length // QB
        lo = max(0, i - blocks // 2)
        n = (i + 1 - lo) * QB
        qrows = slice(i * QB, (i + 1) * QB)
        keys = slice(lo * QB, (i + 1) * QB)
        seg = seg_ref[s:s + 1, :].astype(F32)
        qseg = jnp.broadcast_to(seg[:, qrows], (128, QB)).T
        for t in range(n // 128):
            at = lo * QB + t * 128
            kseg = jnp.broadcast_to(seg[:, at:at + 128], (QB, 128))
            qpos = i * QB + lax.broadcasted_iota(jnp.int32, (QB, 128), 0)
            kpos = at + lax.broadcasted_iota(jnp.int32, (QB, 128), 1)
            ok = (kpos <= qpos) & (kseg == qseg)
            bias[:, t * 128:(t + 1) * 128] = jnp.where(ok, 0.0, MASKED)

        @pl.loop(0, heads // 2)
        def _(pr):
            lanes = pl.ds(pl.multiple_of(pr * 128, 128), 128)
            qb, cb = qs[qrows, lanes], cg[qrows, lanes]
            out, dq = [], []
            for hh in range(2):
                h = pr * 2 + hh
                hr = pl.ds(pl.multiple_of(h * HEAD, HEAD), HEAD)
                km, vm = kmask[h, keys, :], vmask[h, keys, :]
                sc = dot_nt(qb, km) + bias[:, :n]
                e = jnp.exp(sc - jnp.max(sc, axis=1, keepdims=True))
                p = e * (1.0 / jnp.sum(e, axis=1, keepdims=True))
                plow = p.astype(BF)
                out.append(dot(plow, vm))
                dprob = dot_nt(cb, vm)
                delta = jnp.sum(p * dprob, axis=1, keepdims=True)
                ds = (p * (dprob - delta)).astype(BF)
                dq.append(dot(ds, km))
                dvT[hr, keys] += dot(cgT[hr, qrows], plow)
                dkT[hr, keys] += dot(qT[hr, qrows], ds)
            at = slice(s * length + i * QB, s * length + (i + 1) * QB)
            ctx[at, lanes] = (out[0] + out[1]).astype(BF)
            u = (dq[0] + dq[1]) * (HEAD ** -0.5)
            u = u * cos_ref[qrows, :] - pair_swap(u) * sin_ref[qrows, :]
            pg[at, lanes] = u.astype(BF)

    def key_grads(s):
        @pl.loop(0, length // 256)
        def _(i):
            r = pl.ds(pl.multiple_of(i * 256, 256), 256)
            dst = pl.ds(pl.multiple_of(s * length + i * 256, 256), 256)
            c, sn = cos_ref[r, :], sin_ref[r, :]
            for pr in range(heads // 2):
                u = dkT[pr * 128:(pr + 1) * 128, r].T
                u = u * c - pair_swap(u) * sn
                pg[dst, local + pr * 128:local + (pr + 1) * 128] = u.astype(BF)
                u = dvT[pr * 128:(pr + 1) * 128, r].T
                pg[dst, 2 * local + pr * 128:2 * local + (pr + 1) * 128] = u.astype(BF)
            part = pg[dst, :].astype(F32)
            bacc[8:16, 0:3 * local] += jnp.sum(part.reshape(32, 8, 3 * local), axis=0)

    def mix_rows(rb):
        r = slice(rb * QB, (rb + 1) * QB)
        pt[rb] = (dot(act[r, :], w2[...]) + dot(ctx[r, :], wd[...])).astype(BF)
        new_rows(0, rb)

    def grad_rows(rb):
        while not row_sums[(0, rb)].done:
            clock.advance()
        r = slice(rb * QB, (rb + 1) * QB)
        pt[rb] = (dot_nt(dh[r, :], w1[...]) + dot_nt(pg[r, :], wqkv[...])).astype(BF)
        new_rows(1, rb)

    per_seq = length // QB
    work = []

    def add(cost, fn, *args):
        work.append((cost, functools.partial(fn, *args)))

    add(4.0, norm_forward)
    add(1.0, cotangent_sum)
    for j in range(nf):
        add(3.0, feed_forward, j, 0, rows)
        add(1.3, fc2_chunk, j)
    for s in range(seqs):
        add(2.5, project, s)
        add(1.0, context_grad, s)
        for i in range(per_seq):
            add(1.0 + min(i, 2), attend, s, i)
            rb = s * per_seq + i
            add(1.0, mix_rows, rb)
            y_order.append((0, rb))
        add(1.0, key_grads, s)
        for j in range(2):
            if s * 2 + j < nf:
                add(1.3, fc1_chunk, s * 2 + j)
        for i in range(per_seq):
            rb = s * per_seq + i
            add(1.5, grad_rows, rb)
            y_order.append((1, rb))
    for j in range(width // 256):
        add(1.0, qkv_chunk, j)
    add(0.5, dense_chunk)

    fetch(0)
    pl.semaphore_wait(barrier, len(dp_devs) + 2)
    for cost, fn in work:
        clock.run(cost, fn)
    clock.drain()
    for chunk in chunks:
        chunk.finish()
    for item in row_sums.values():
        item.finish()
    norm_finish()


def fused_layer(x, g, wqkv, wd, w1, w2, seg, gain, lnb, bqkv, db, b1, b2, cos, sin):
    rows, width = x.shape
    local, ff = wd.shape[0], w1.shape[1]
    length = seg.shape[1]
    heads = local // HEAD
    nf, nw, nrb = ff // 256, width // 256, rows // 256
    nchunk = 2 * nf + nw + 1
    extra = 32
    any_spec, vmem = pl.BlockSpec(memory_space=pl.ANY), pl.BlockSpec(memory_space=pltpu.VMEM)

    def buf(*shape, dtype=BF):
        return pltpu.VMEM(shape, dtype)

    nA, hd = 2 * nf, (local + extra) // 2
    scratch = [
        buf(rows, width), buf(rows, width), buf(rows, ff), buf(rows, ff),
        buf(width, 3 * local), buf(local, width), buf(width, ff), buf(ff, width),
        buf(length, local), buf(heads, length, 128), buf(heads, length, 128), buf(local, length),
        buf(length, local), buf(local, length), buf(rows, local), buf(rows, 3 * local),
        buf(local, length, dtype=F32), buf(local, length, dtype=F32),
        buf(256, length // 2 + 256, dtype=F32), buf(16, width, dtype=F32), buf(24, width, dtype=F32),
        buf(nrb, 256, width), buf(nrb, 128, width), buf(nrb, 128, width), buf(2, 128, width),
        buf(nA, 256, width), buf(nw, 256, 3 * local), buf(local + extra, width),
        buf(nA, 128, width), buf(nA, 128, width), buf(nA, 128, width),
        buf(nw, 128, 3 * local), buf(nw, 128, 3 * local), buf(nw, 128, 3 * local),
        buf(hd, width), buf(hd, width), buf(hd, width),
        buf(8, width // 4, dtype=F32), buf(8, width // 4, dtype=F32),
        buf(GROUP - 1, 8, width // 4, dtype=F32),
        pltpu.SemaphoreType.DMA((9,)), pltpu.SemaphoreType.DMA((2,)),
        pltpu.SemaphoreType.DMA((nchunk, 5)), pltpu.SemaphoreType.DMA((nchunk, 4)),
        pltpu.SemaphoreType.DMA((2 * nrb, 4)), pltpu.SemaphoreType.DMA((2 * nrb, 3)),
        pltpu.SemaphoreType.DMA((GROUP,)), pltpu.SemaphoreType.DMA((GROUP,)),
        pltpu.SemaphoreType.REGULAR((nrb,)),
    ]
    out_shape = [
        jax.ShapeDtypeStruct((rows, width), BF),
        jax.ShapeDtypeStruct((rows, width), BF),
        jax.ShapeDtypeStruct((ff, width), BF),
        jax.ShapeDtypeStruct((width, ff), BF),
        jax.ShapeDtypeStruct((width, 3 * local), BF),
        jax.ShapeDtypeStruct((local + extra, width), BF),
        jax.ShapeDtypeStruct((8, width // 4), F32),
    ]
    macs = rows * width * (6 * ff + 9 * local) + 12 * heads * rows * length * HEAD
    return pl.pallas_call(
        layer_kernel,
        out_shape=out_shape,
        in_specs=[any_spec] * 6 + [vmem] * 9,
        out_specs=[any_spec] * 6 + [vmem],
        scratch_shapes=scratch,
        compiler_params=pltpu.CompilerParams(
            collective_id=0, has_side_effects=True, vmem_limit_bytes=63 * 2**20
        ),
        cost_estimate=pl.CostEstimate(
            flops=2 * macs, bytes_accessed=40 * 2**20, transcendentals=heads * rows * length
        ),
        name="layer",
    )(x, g, wqkv, wd, w1, w2, seg, gain, lnb, bqkv, db, b1, b2, cos, sin)


def local_part(
    n_dp, tokens, segment_ids, ln_gain, ln_bias, qkv_weight, qkv_bias, dense_weight, dense_bias,
    fc1_weight, fc1_bias, fc2_weight, fc2_bias, cotangent,
):
    width = tokens.shape[1]
    local = qkv_weight.shape[2]
    cos, sin = rotary_tables(segment_ids.shape[1])
    outs = fused_layer(
        tokens, cotangent, qkv_weight.reshape(width, 3 * local), dense_weight, fc1_weight, fc2_weight,
        segment_ids, ln_gain[None], ln_bias[None], qkv_bias.reshape(1, 3 * local), dense_bias[None],
        fc1_bias[None], fc2_bias[None], cos, sin,
    )
    mixed, igrad, sums = outs[0], outs[1], list(outs[2:])
    if n_dp > GROUP:
        groups = [[k + GROUP * j for j in range(n_dp // GROUP)] for k in range(GROUP)]
        sums = [lax.psum(s, "dp", axis_index_groups=groups) for s in sums]
    fc2, fc1, qkv, dense, norm = sums
    out_bias = dense[local + 2].astype(F32)
    return (
        mixed,
        igrad,
        norm[0:4].reshape(width),
        norm[4:8].reshape(width),
        qkv.astype(F32).reshape(width, 3, local),
        dense[local + 1, :3 * local].astype(F32).reshape(3, local),
        dense[:local].astype(F32),
        out_bias,
        fc1.astype(F32),
        dense[local, :fc1_bias.shape[0]].astype(F32),
        fc2.astype(F32),
        out_bias,
    )


def solution(mesh):
    row, whole = P("dp", None), P()
    weights = (
        whole, whole, P(None, None, "tensor"), P(None, "tensor"), P("tensor", None), whole,
        P(None, "tensor"), P("tensor"), P("tensor", None), whole,
    )
    return jax.shard_map(
        functools.partial(local_part, mesh.shape["dp"]),
        mesh=mesh,
        in_specs=(row, row) + weights + (row,),
        out_specs=(row, row) + weights,
        check_vma=False,
    )
```

```python
import functools
import heapq

import jax
import jax.numpy as jnp
import numpy as np
from jax import lax
from jax.experimental import pallas as pl
from jax.experimental.pallas import tpu as pltpu
from jax.sharding import PartitionSpec as P

HEAD = 64
ROTARY = 32
NORM_EPS = 1e-05
MASKED = -1e30
BASE = 10000.0
BF = jnp.bfloat16
F32 = jnp.float32
MESH = pl.DeviceIdType.MESH
GROUP = 8

ORDER = (
    ("LN", 0), ("FF", 1, 0), ("FF", 0, 0), ("LN", 1), ("CG", 0, 0), ("LN", 2), ("CG", 0, 1), ("LN", 3), ("FF", 2, 2),
    ("FF", 0, 3), ("FF", 0, 1), ("FF", 2, 1), ("FF", 1, 1), ("FF", 1, 2), ("FF", 3, 3), ("FF", 0, 2), ("FF", 3, 1),
    ("PROJ", 0, 1), ("FC2", 0), ("PROJ", 0, 0), ("FF", 2, 3), ("FF", 3, 2), ("FF", 3, 0), ("FF", 1, 3), ("FF", 2, 0),
    ("FC1", 3), ("ATT", 0, 1), ("MIX", 1), ("FC1", 1), ("FC2", 1), ("ATT", 0, 3), ("ATT", 0, 0), ("MIX", 0),
    ("MIX", 3), ("FC2", 3), ("ATT", 0, 2), ("MIX", 2), ("KEY", 0), ("FC2", 2), ("CG", 1, 0), ("GRAD", 1), ("FC1", 0),
    ("GRAD", 0), ("PROJ", 1, 1), ("PROJ", 1, 0), ("FC1", 2), ("GRAD", 3), ("ATT", 1, 1), ("MIX", 5), ("COT",),
    ("ATT", 1, 0), ("CG", 1, 1), ("MIX", 4), ("ATT", 1, 2), ("MIX", 6), ("ATT", 1, 3), ("MIX", 7), ("KEY", 1),
    ("QKV", 0), ("GRAD", 5), ("DENSE",), ("QKV", 1), ("QKV", 2), ("GRAD", 4), ("BIAS",), ("GRAD", 7), ("GRAD", 2),
    ("GRAD", 6),
)
KINDS = {
    ("FC2", 0): "AA", ("FC2", 1): "AA", ("FC2", 2): "AA", ("FC2", 3): "BA", ("FC1", 0): "BB", ("FC1", 1): "BA",
    ("FC1", 2): "AA", ("FC1", 3): "AA", ("QKV", 0): "AB", ("QKV", 1): "AA", ("QKV", 2): "AA", ("DENSE",): "AB",
}


def dot(a, b):
    return lax.dot_general(a, b, (((1,), (0,)), ((), ())), preferred_element_type=F32)


def dot_nt(a, b):
    return lax.dot_general(a, b, (((1,), (1,)), ((), ())), preferred_element_type=F32)


def dot_tn(a, b):
    return lax.dot_general(a, b, (((0,), (0,)), ((), ())), preferred_element_type=F32)


def rotary_tables(length):
    half = ROTARY // 2
    frequency = (BASE ** (-(np.arange(half, dtype=np.float32) * 2.0) / ROTARY)).astype(np.float32)
    angles = np.arange(length, dtype=np.float32)[:, None] * frequency[None, :]
    cosine, sine = np.cos(angles), np.sin(angles)
    rest = HEAD - ROTARY
    c = np.concatenate([cosine, cosine, np.ones((length, rest), np.float32)], axis=1)
    s = np.concatenate([-sine, sine, np.zeros((length, rest), np.float32)], axis=1)
    return np.tile(c, (1, 2)).astype(np.float32), np.tile(s, (1, 2)).astype(np.float32)


def pair_swap(u):
    lane = lax.broadcasted_iota(jnp.int32, u.shape, 1)
    half = ROTARY // 2
    return jnp.where(lane % ROTARY < half, pltpu.roll(u, 128 - half, 1), pltpu.roll(u, half, 1))


class Clock:
    UNIT_KIB = 128
    UNIT_US = 2.8
    CORE_US = 0.4
    LATENCY = 2.2
    MARGIN = 0.5
    STEP_US = 0.1
    ADD_US = 0.03

    def __init__(self):
        self.now = 0.0
        self.queue = []
        self.count = 0
        self.free = {}

    def at(self, when, step):
        heapq.heappush(self.queue, (when, self.count, step))
        self.count += 1

    def arrival(self, link, units):
        start = max(self.now, self.free.get(link, 0.0))
        self.free[link] = start + units * (self.CORE_US if link == "core" else self.UNIT_US)
        return self.free[link] + self.LATENCY + self.MARGIN

    def spend(self, adds=0.0, more=0.0):
        self.now += self.STEP_US + self.ADD_US * adds + more

    def advance(self):
        when, _, step = heapq.heappop(self.queue)
        self.now = max(self.now, when)
        step()

    def due(self):
        while self.queue and self.queue[0][0] <= self.now:
            self.advance()

    def drain(self):
        while self.queue:
            self.advance()


def layer_kernel(
    x_hbm, g_hbm, wqkv_hbm, wd_hbm, w1_hbm, w2_hbm,
    seg_ref, gain_ref, lnb_ref, bqkv_ref, db_ref, b1_ref, b2_ref, cos_ref, sin_ref,
    mixed_hbm, igrad_hbm, fc2_hbm, fc1_hbm, qkv_hbm, dense_hbm, norm_out, bias_out,
    nb, gb, act, dh, wqkv, wd, w1, w2,
    qs, ks, vs, qT, cg, ctx, pg, dkT, dvT, bias, gacc, bacc,
    s0, s1, d0, d1,
    pt, t1r, t2r, xs, gA, gQ, gD, rA, rQ, rD,
    norm_send, norm_core, norm_recv, bias_send, bias_recv,
    load_sem, x_sem, dp_send, dp_recv, t_send, t_recv, sm_send, sm_recv, credit,
):
    rows, width = nb.shape
    seqs, length = seg_ref.shape
    local = wd.shape[0]
    ff = w1.shape[1]
    heads = local // HEAD
    QB = 256
    nrb = rows // QB
    HB = QB // 2

    dp, tensor = lax.axis_index("dp"), lax.axis_index("tensor")
    base = dp - lax.rem(dp, GROUP)
    me = lax.rem(dp, GROUP)
    xx, zz = lax.rem(me, 2), me // 2
    yy, cc = tensor // 2, lax.rem(tensor, 2)
    x_dev = (base + zz * 2 + (1 - xx), tensor)
    pair_dev = (base + (zz + 1 - 2 * lax.rem(zz, 2)) * 2 + xx, tensor)
    mid_dev = (base + (3 - zz) * 2 + xx, tensor)
    y_dev = (dp, (1 - yy) * 2 + cc)
    c_dev = (dp, yy * 2 + (1 - cc))
    side = zz // 2
    inner = (zz == 1) | (zz == 2)
    outer = jnp.logical_not(inner)
    dp_devs = [(base + lax.rem(me + k, GROUP), tensor) for k in range(1, GROUP)]

    barrier = pltpu.get_barrier_semaphore()
    for device in dp_devs + [y_dev, c_dev]:
        pl.semaphore_signal(barrier, inc=1, device_id=device, device_id_type=MESH)

    loads = {}

    def load(name, src, dst):
        loads[name] = pltpu.make_async_copy(src, dst, load_sem.at[len(loads)])
        loads[name].start()

    quarter = rows // 4
    parts = [pl.ds(k * quarter, quarter) for k in range(4)]
    load("x0", x_hbm.at[parts[0]], act.at[parts[0]])
    load("w1", w1_hbm, w1)
    load("w2", w2_hbm, w2)
    load("g0", g_hbm.at[parts[0]], gb.at[parts[0]])
    for k in range(1, 4):
        load(f"x{k}", x_hbm.at[parts[k]], act.at[parts[k]])
        load(f"g{k}", g_hbm.at[parts[k]], gb.at[parts[k]])
    for k in range(3):
        load(f"wqkv{k}", wqkv_hbm.at[k], wqkv.at[:, k * local:(k + 1) * local])
    load("wd", wd_hbm, wd)
    for ref in (bacc, gacc, dkT, dvT):
        ref[...] = jnp.zeros_like(ref)

    clock = Clock()
    cgT = gD.at[:, pl.ds(0, length)]
    prob_low = [[gQ.at[j, pl.ds(k * QB, QB)] for j in range(3)] for k in range(4)]

    def remote(src, dst, send_sem, recv_sem, device):
        return pltpu.make_async_remote_copy(
            src_ref=src, dst_ref=dst, send_sem=send_sem, recv_sem=recv_sem,
            device_id=device, device_id_type=MESH,
        )

    def span(first, n):
        return pl.ds(pl.multiple_of(first, 16), n)

    def add_rows(dst, a_ref, b_ref):
        n, cols = dst.shape
        step = min(n, 65536 // cols)
        if n % step:
            step = 48

        @pl.loop(0, n // step)
        def _(k):
            r = span(k * step, step)
            dst[r, :] = a_ref[r, :] + b_ref[r, :]

    class PairFirst:
        def __init__(self, k, own, got, out, out_row):
            h = own.shape[0] // 2
            self.h, self.units = h, h * own.shape[1] * 2 / 1024 / clock.UNIT_KIB
            self.xr, self.zi, self.zm = (got.at[pl.ds(j * h, h)] for j in range(3))
            self.keep = own.at[span(xx * h, h)]
            target = out.at[span(out_row + xx * h, h)]
            send, recv = dp_send.at[k], dp_recv.at[k]
            self.c_x = remote(own.at[span((1 - xx) * h, h)], self.xr, send.at[0], recv.at[0], x_dev)
            self.c_in = remote(self.xr, self.zi, send.at[1], recv.at[1], pair_dev)
            self.c_mid = remote(self.zi, self.zm, send.at[2], recv.at[2], mid_dev)
            self.c_out = remote(self.zm, self.zm, send.at[1], recv.at[2], pair_dev)
            self.c_ag = remote(self.zm, target, send.at[3], recv.at[3], x_dev)
            self.c_loc = pltpu.make_async_copy(self.zm, target, send.at[4])

        def start(self):
            self.c_x.start()
            clock.spend()
            clock.at(clock.arrival("x", self.units), self.pair_sum)

        def pair_sum(self):
            self.c_x.wait_recv()
            add_rows(self.xr, self.xr, self.keep)

            @pl.when(outer)
            def _():
                self.c_in.start()

            clock.spend(self.units)
            clock.at(clock.arrival("zin", self.units), self.side_sum)

        def side_sum(self):
            @pl.when(inner)
            def _():
                self.c_in.wait_recv()
                add_rows(self.zi, self.zi, self.xr)
                self.c_mid.start()

            clock.spend(self.units)
            clock.at(clock.arrival("zmid", self.units), self.line_sum)

        def line_sum(self):
            @pl.when(inner)
            def _():
                self.c_mid.wait_recv()
                self.c_mid.wait_send()
                add_rows(self.zm, self.zm, self.zi)
                self.c_out.start()
                self.c_ag.start()
                self.c_loc.start()

            clock.spend(self.units)
            clock.at(clock.arrival("zout", self.units), self.outer_end)

        def outer_end(self):
            @pl.when(outer)
            def _():
                self.c_mid.wait_recv()
                self.c_ag.start()
                self.c_loc.start()

            clock.spend()
            clock.arrival("x", self.units)

        def finish(self):
            self.c_x.wait_send()
            self.c_in.wait_send()
            self.c_ag.wait()
            self.c_loc.wait()

    class LineFirst:
        def __init__(self, k, own, got, out, out_row):
            n = own.shape[0]
            b = n // 4
            self.b, self.units = b, b * own.shape[1] * 2 / 1024 / clock.UNIT_KIB
            self.r1, self.r2, self.xb = got.at[pl.ds(0, 3 * b)], got.at[pl.ds(3 * b, 2 * b)], got.at[pl.ds(5 * b, b)]
            rest = own.at[span((1 - side) * b, 3 * b)]
            self.mine = own.at[span(zz * b, b)]
            self.far = own.at[span((1 - side) * 2 * b, 2 * b)]
            near = own.at[span(side * 2 * b, 2 * b)]
            self.outers = own.at[span(side * 3 * b, b)]
            self.r1_far = self.r1.at[span((1 - side) * b, 2 * b)]
            self.r1_mine = self.r1.at[span(side * 2 * b, b)]
            self.r2_mine = self.r2.at[span((1 - side) * b, b)]
            self.r2_outer = self.r2.at[span(side * b, b)]
            r1_first = self.r1.at[pl.ds(0, b)]
            self.r1_first = r1_first
            send, recv = dp_send.at[k], dp_recv.at[k]
            self.c_1 = remote(rest, self.r1, send.at[0], recv.at[0], pair_dev)
            self.c_2 = remote(self.r1_far, self.r2, send.at[0], recv.at[1], mid_dev)
            self.c_3 = remote(self.r2_outer, r1_first, send.at[1], recv.at[0], pair_dev)
            self.c_x = remote(self.mine, self.xb, send.at[2], recv.at[2], x_dev)
            self.c_5 = remote(self.mine, self.mine, send.at[1], recv.at[3], pair_dev)
            self.c_5r = remote(self.outers, self.outers, send.at[1], recv.at[3], pair_dev)
            self.c_6 = remote(near, near, send.at[3], recv.at[1], mid_dev)
            self.c_6r = remote(self.far, self.far, send.at[3], recv.at[1], mid_dev)
            self.c_7 = remote(rest, rest, send.at[4], recv.at[3], pair_dev)
            self.c_loc = pltpu.make_async_copy(own, out.at[span(out_row, n)], send.at[5])

        def start(self):
            @pl.when(outer)
            def _():
                self.c_1.start()

            clock.spend(2 * self.units)
            clock.at(clock.arrival("zin", 3 * self.units), self.side_sum)

        def side_sum(self):
            @pl.when(inner)
            def _():
                self.c_1.wait_recv()
                add_rows(self.r1_far, self.r1_far, self.far)
                self.c_2.start()
                add_rows(self.r1_mine, self.r1_mine, self.mine)

            clock.spend(2 * self.units)
            clock.at(clock.arrival("zmid", 2 * self.units), self.line_sum)

        def line_sum(self):
            @pl.when(inner)
            def _():
                self.c_2.wait_recv()
                add_rows(self.r2_outer, self.r2_outer, self.outers)
                self.c_3.start()
                add_rows(self.mine, self.r1_mine, self.r2_mine)
                self.c_x.start()

            clock.spend(2 * self.units)
            clock.at(clock.arrival("zout", self.units), self.outer_sum)

        def outer_sum(self):
            @pl.when(outer)
            def _():
                self.c_3.wait_recv()
                add_rows(self.mine, self.mine, self.r1_first)
                self.c_x.start()

            clock.spend(2 * self.units)
            clock.at(clock.arrival("x", self.units), self.pair_sum)

        def pair_sum(self):
            self.c_x.wait()
            add_rows(self.mine, self.mine, self.xb)

            @pl.when(outer)
            def _():
                self.c_1.wait_send()
                self.c_5.start()

            clock.spend(2 * self.units)
            clock.at(clock.arrival("zin", self.units), self.side_gather)

        def side_gather(self):
            @pl.when(inner)
            def _():
                self.c_5r.wait_recv()
                self.c_6.start()

            clock.spend(2 * self.units)
            clock.at(clock.arrival("zmid", 2 * self.units), self.line_gather)

        def line_gather(self):
            @pl.when(inner)
            def _():
                self.c_6r.wait_recv()
                self.c_7.start()
                self.c_loc.start()

            clock.spend(2 * self.units)
            clock.at(clock.arrival("zout", 3 * self.units), self.outer_end)

        def outer_end(self):
            @pl.when(outer)
            def _():
                self.c_7.wait_recv()
                self.c_loc.start()

        def finish(self):
            @pl.when(outer)
            def _():
                self.c_5.wait_send()

            @pl.when(inner)
            def _():
                self.c_2.wait_send()
                self.c_3.wait_send()
                self.c_6.wait_send()
                self.c_7.wait_send()

            self.c_loc.wait()

    chunks = []

    kind_of = {"A": PairFirst, "B": LineFirst}

    def new_chunk(own, got, out, out_row, kinds):
        n, m = own.shape[0] // len(kinds), got.shape[0] // len(kinds)
        for k, kind in enumerate(kinds):
            part = own.at[pl.ds(k * n, n)]
            chunk = kind_of[kind](len(chunks), part, got.at[pl.ds(k * m, m)], out, out_row + k * n)
            chunks.append(chunk)
            chunk.start()

    y_order = []
    mine = span(cc * HB, HB)
    other = span((1 - cc) * HB, HB)

    def fetch(seq):
        if seq < len(y_order):
            rb = y_order[seq][1]
            src = x_hbm.at[span(rb * QB + cc * HB, HB)]
            pltpu.make_async_copy(src, xs.at[seq % 2], x_sem.at[seq % 2]).start()

    def row_stats(x):
        mu = jnp.mean(x, axis=1, keepdims=True)
        cent = x - mu
        rstd = lax.rsqrt(jnp.mean(cent * cent, axis=1, keepdims=True) + NORM_EPS)
        return cent * rstd, rstd

    class RowSum:
        def __init__(self, phase, rb):
            self.phase, self.rb, self.done = phase, rb, False
            k = phase * nrb + rb
            out = igrad_hbm if phase else mixed_hbm
            target = out.at[span(rb * QB + cc * HB, HB)]
            self.own = own = pt.at[rb, mine]
            self.units = HB * width * 2 / 1024 / clock.UNIT_KIB
            send, recv = t_send.at[k], t_recv.at[k]
            self.c_core = remote(pt.at[rb, other], t1r.at[rb], send.at[0], recv.at[0], c_dev)
            self.c_y = remote(own, t2r.at[rb], send.at[1], recv.at[1], y_dev)
            self.c_fin = remote(t2r.at[rb], target, send.at[2], recv.at[2], c_dev)
            self.c_loc = pltpu.make_async_copy(t2r.at[rb], target, send.at[3])

        def start(self):
            if self.phase:
                before = row_sums[(0, self.rb)]
                before.c_fin.wait_recv()
            self.c_core.start()
            clock.spend()
            clock.at(clock.arrival("core", self.units), self.chip_sum)

        def chip_sum(self):
            self.c_core.wait_recv()
            add_rows(self.own, self.own, t1r.at[self.rb])
            if self.phase:
                pl.semaphore_wait(credit.at[self.rb], 1)
            self.c_y.start()
            clock.spend(self.units)
            clock.at(clock.arrival("y", self.units), self.whole_sum)

        def whole_sum(self):
            rb = self.rb
            seq = y_order.index((self.phase, rb))
            slot = seq % 2
            fetch(seq + 1)
            pltpu.make_async_copy(x_hbm.at[pl.ds(0, HB)], xs.at[slot], x_sem.at[slot]).wait()
            self.c_y.wait_recv()
            step, group = 16, 4
            own, arrived = self.own, t2r.at[rb]

            @pl.loop(0, HB // (step * group))
            def _(k):
                for j in range(group):
                    first = (k * group + j) * step
                    r = span(first, step)
                    x = xs[slot, r, :].astype(F32)
                    total = own[r, :].astype(F32) + arrived[r, :].astype(F32)
                    if self.phase == 0:
                        arrived[r, :] = (x + total + (db_ref[...] + b2_ref[...])).astype(BF)
                    else:
                        xhat, rstd = row_stats(x)
                        gacc[0:8, :] += jnp.sum((total * xhat).reshape(step // 8, 8, width), axis=0)
                        gacc[8:16, :] += jnp.sum(total.reshape(step // 8, 8, width), axis=0)
                        e = total * gain_ref[...]
                        m1 = jnp.mean(e, axis=1, keepdims=True)
                        m2 = jnp.mean(e * xhat, axis=1, keepdims=True)
                        gr = span(rb * QB + cc * HB + first, step)
                        grad = gb[gr, :].astype(F32) + rstd * (e - m1 - xhat * m2)
                        arrived[r, :] = grad.astype(BF)

            self.c_fin.start()
            self.c_loc.start()
            clock.spend(0, 0.6 if self.phase else 0.35)
            if self.phase == 0:
                clock.at(clock.now + 4.0, self.give_back)
            elif seq == len(y_order) - 1:
                clock.at(clock.now, norm_sums)

        def give_back(self):
            clock.spend()
            self.c_fin.wait_send()
            self.c_loc.wait()
            self.c_core.wait_send()
            self.c_y.wait_send()
            pl.semaphore_signal(credit.at[self.rb], inc=1, device_id=y_dev, device_id_type=MESH)
            self.done = True

        def finish(self):
            if self.phase:
                self.c_core.wait_send()
                self.c_y.wait_send()
                self.c_fin.wait()
                self.c_loc.wait()

    row_sums = {}

    def new_rows(phase, rb):
        row_sums[(phase, rb)] = RowSum(phase, rb)
        row_sums[(phase, rb)].start()

    small = []

    def fold(dst, first, line):
        for k in range(line.shape[1] // 128):
            dst[first + k:first + k + 1, :] = line[:, k * 128:(k + 1) * 128]

    def send_small(src, slots, first_sem):
        for k, device in enumerate(dp_devs):
            sem = first_sem + k
            copy = remote(src, slots.at[k], sm_send.at[sem], sm_recv.at[sem], device)
            copy.start()
            small.append(copy)

    def sum_small(src, slots):
        total = jnp.zeros(src.shape, F32)
        for place in range(GROUP):
            behind = lax.rem(me - place + GROUP, GROUP)
            there = slots[jnp.maximum(behind - 1, 0)]
            total = total + jnp.where(behind == 0, src[...], there)
        return total

    def bias_sums():
        for k in range(3):
            fold(bias_send, 8 * k, jnp.sum(bacc[8 * k:8 * k + 8, :], axis=0, keepdims=True))
        send_small(bias_send, bias_recv, 1)

    def norm_sums():
        for k in range(2):
            fold(norm_send, 8 * k, jnp.sum(gacc[8 * k:8 * k + 8, :], axis=0, keepdims=True))
        swap = remote(norm_send, norm_core, sm_send.at[0], sm_recv.at[0], c_dev)
        swap.start()
        swap.wait()
        norm_send[...] = norm_send[...] + norm_core[...]
        send_small(norm_send, norm_recv, GROUP)

    def small_finish():
        for copy in small:
            copy.wait()
        norm_out[...] = sum_small(norm_send, norm_recv)
        bias_out[...] = sum_small(bias_send, bias_recv)

    def wait_load(*names):
        for name in names:
            if name in loads:
                loads.pop(name).wait()

    def norm_forward(k):
        step, group = 16, 8
        wait_load(f"x{k}")

        @pl.loop(k * quarter // (step * group), (k + 1) * quarter // (step * group))
        def _(i):
            for j in range(group):
                r = span((i * group + j) * step, step)
                xhat, _ = row_stats(act[r, :].astype(F32))
                nb[r, :] = (xhat * gain_ref[...] + lnb_ref[...]).astype(BF)

    def cotangent_sum():
        wait_load("g0", "g1", "g2", "g3")
        step = 64

        @pl.loop(0, rows // step)
        def _(i):
            r = span(i * step, step)
            bacc[16:24, :] += jnp.sum(gb[r, :].astype(F32).reshape(step // 8, 8, width), axis=0)

    def ff_products(j, q, slot):
        wait_load("w1", "w2", f"g{q}")
        cols, r = slice(j * 256, (j + 1) * 256), slice(q * quarter, (q + 1) * quarter)
        h = dot(nb[r, :], w1[:, cols])
        up = dot_nt(gb[r, :], w2[cols, :])
        for k in range(quarter // 256):
            (s0, s1)[slot][:, k * 256:(k + 1) * 256] = h[k * 256:(k + 1) * 256]
            (d0, d1)[slot][:, k * 256:(k + 1) * 256] = up[k * 256:(k + 1) * 256]

    def ff_gelu(j, q, slot):
        cols = slice(j * 256, (j + 1) * 256)
        step = 32
        k0 = 0.7978845608028654
        for t in range(quarter // step):
            at = slice(t * step % 256, t * step % 256 + step)
            lane = slice(t * step // 256 * 256, t * step // 256 * 256 + 256)
            r = slice(q * quarter + t * step, q * quarter + (t + 1) * step)
            h = (s0, s1)[slot][at, lane] + b1_ref[:, cols]
            up = (d0, d1)[slot][at, lane]
            h2 = h * h
            th = jnp.tanh(k0 * h * (1.0 + 0.044715 * h2))
            half = 0.5 * (1.0 + th)
            act[r, cols] = (h * half).astype(BF)
            slope = half + 0.5 * h * (1.0 - th * th) * (k0 * (1.0 + 3 * 0.044715 * h2))
            hg = (up * slope).astype(BF)
            dh[r, cols] = hg
            bacc[0:8, cols] += jnp.sum(hg.astype(F32).reshape(step // 8, 8, 256), axis=0)

    ahead = {"slot": 0, "ready": False}

    def feed_forward(j, q, following=None):
        slot = ahead["slot"]
        if not ahead["ready"]:
            ff_products(j, q, slot)
        if following:
            ff_products(*following, 1 - slot)
        ahead["slot"], ahead["ready"] = 1 - slot, bool(following)
        ff_gelu(j, q, slot)

    nf = ff // 256

    def fc2_chunk(j, kind):
        wait_load("g0", "g1", "g2", "g3")
        gA[j] = dot_tn(act[:, j * 256:(j + 1) * 256], gb[...]).astype(BF)
        new_chunk(gA.at[j], rA.at[j], fc2_hbm, j * 256, kind)

    def fc1_chunk(j, kind):
        k = nf + j
        gA[k] = dot_tn(nb[:, j * 256:(j + 1) * 256], dh[...]).astype(BF)
        new_chunk(gA.at[k], rA.at[k], fc1_hbm, j * 256, kind)

    def qkv_chunk(j, kind):
        for k in range(2):
            at = slice(k * width // 2, (k + 1) * width // 2)
            gQ[j, at, :] = dot_tn(nb[:, at], pg[:, j * local:(j + 1) * local]).astype(BF)
        new_chunk(gQ.at[j], rQ.at[j], qkv_hbm.at[j], 0, kind)

    def dense_chunk(kind):
        gD[...] = dot_tn(ctx[...], gb[...]).astype(BF)
        new_chunk(gD, rD, dense_hbm, 0, kind)

    def project(s, half):
        wait_load("wqkv0", "wqkv1", "wqkv2")
        for i in range(half * length // 512, (half + 1) * length // 512):
            r = slice(i * 256, (i + 1) * 256)
            src = slice(s * length + i * 256, s * length + (i + 1) * 256)
            c, sn = cos_ref[r, :], sin_ref[r, :]
            for part in range(3):
                y = dot(nb[src, :], wqkv[:, part * local:(part + 1) * local]) + bqkv_ref[part:part + 1, :]
                for pr in range(heads // 2):
                    lanes = slice(pr * 128, (pr + 1) * 128)
                    u = y[:, lanes]
                    if part < 2:
                        u = u * c + pair_swap(u) * sn
                    if part == 0:
                        u = u * (HEAD ** -0.5)
                        qT[lanes, r] = u.T.astype(BF)
                    (qs, ks, vs)[part][r, lanes] = u.astype(BF)

    def context_grad(s, half):
        wait_load("wd", f"g{2 * s + half}")
        r = slice(half * length // 2, (half + 1) * length // 2)
        u = dot_nt(gb[s * length + half * length // 2:s * length + (half + 1) * length // 2, :], wd[...])
        cg[r, :] = u.astype(BF)
        cgT[:, r] = u.T.astype(BF)

    def attend(s, i):
        blocks = length // QB
        lo = max(0, i - blocks // 2)
        n = (i + 1 - lo) * QB
        qrows = slice(i * QB, (i + 1) * QB)
        keys = slice(lo * QB, (i + 1) * QB)
        at_rows = slice(s * length + i * QB, s * length + (i + 1) * QB)
        seg = seg_ref[s:s + 1, :].astype(F32)
        qseg = jnp.broadcast_to(seg[:, qrows], (128, QB)).T
        for t in range(n // 128):
            at = lo * QB + t * 128
            kseg = jnp.broadcast_to(seg[:, at:at + 128], (QB, 128))
            qpos = i * QB + lax.broadcasted_iota(jnp.int32, (QB, 128), 0)
            kpos = at + lax.broadcasted_iota(jnp.int32, (QB, 128), 1)
            ok = (kpos <= qpos) & (kseg == qseg)
            bias[:, t * 128:(t + 1) * 128] = jnp.where(ok, 0.0, MASKED)
        low = lax.broadcasted_iota(jnp.int32, (QB, 128), 1) < HEAD
        zero = jnp.zeros((), BF)

        def head_of(u, h):
            return jnp.where(low, u, zero) if h % 2 == 0 else jnp.where(low, zero, u)

        def scores(h):
            lanes = slice(h // 2 * 128, h // 2 * 128 + 128)
            (s0, s1)[h % 2][:, :n] = dot_nt(head_of(qs[qrows, lanes], h), ks[keys, lanes])
            (d0, d1)[h % 2][:, :n] = dot_nt(head_of(cg[qrows, lanes], h), vs[keys, lanes])

        def soft(h):
            step = 16
            sc_ref, dp_ref = (s0, s1)[h % 2], (d0, d1)[h % 2]

            def put(dst, r, value):
                for j in range(n // QB):
                    dst[j][r, :] = value[:, j * QB:(j + 1) * QB]

            for t in range(QB // step):
                r = slice(t * step, (t + 1) * step)
                sc = sc_ref[r, :n] + bias[r, :n]
                e = jnp.exp(sc - jnp.max(sc, axis=1, keepdims=True))
                p = e * (1.0 / jnp.sum(e, axis=1, keepdims=True))
                put(prob_low[h % 2], r, p.astype(BF))
                pd = p * dp_ref[r, :n]
                delta = jnp.sum(pd, axis=1, keepdims=True)
                put(prob_low[2 + h % 2], r, (pd - p * delta).astype(BF))

        def products(h, kept):
            lanes = slice(h // 2 * 128, h // 2 * 128 + 128)
            hr = slice(h * HEAD, (h + 1) * HEAD)
            p, e = (jnp.concatenate([prob_low[k][j][...] for j in range(n // QB)], axis=1) for k in (h % 2, 2 + h % 2))
            kept.append((dot(p, vs[keys, lanes]), dot(e, ks[keys, lanes])))
            dvT[hr, keys] += dot(cgT[hr, qrows], p)
            dkT[hr, keys] += dot(qT[hr, qrows], e)
            if h % 2:
                (o_a, q_a), (o_b, q_b) = kept
                kept.clear()
                ctx[at_rows, lanes] = jnp.where(low, o_a, o_b).astype(BF)
                u = jnp.where(low, q_a, q_b) * (HEAD ** -0.5)
                u = u * cos_ref[qrows, :] - pair_swap(u) * sin_ref[qrows, :]
                pg[at_rows, lanes] = u.astype(BF)

        kept = []
        scores(0)
        for h in range(heads):
            if h + 1 < heads:
                scores(h + 1)
            soft(h)
            products(h, kept)

    def key_grads(s):
        @pl.loop(0, length // 256)
        def _(i):
            r = pl.ds(pl.multiple_of(i * 256, 256), 256)
            dst = pl.ds(pl.multiple_of(s * length + i * 256, 256), 256)
            c, sn = cos_ref[r, :], sin_ref[r, :]
            for pr in range(heads // 2):
                u = dkT[pr * 128:(pr + 1) * 128, r].T
                u = u * c - pair_swap(u) * sn
                pg[dst, local + pr * 128:local + (pr + 1) * 128] = u.astype(BF)
                u = dvT[pr * 128:(pr + 1) * 128, r].T
                pg[dst, 2 * local + pr * 128:2 * local + (pr + 1) * 128] = u.astype(BF)
            part = pg[dst, :].astype(F32)
            bacc[8:16, 0:3 * local] += jnp.sum(part.reshape(32, 8, 3 * local), axis=0)

        dkT[...] = jnp.zeros_like(dkT)
        dvT[...] = jnp.zeros_like(dvT)

    def mix_rows(rb):
        r = slice(rb * QB, (rb + 1) * QB)
        pt[rb] = (dot(act[r, :], w2[...]) + dot(ctx[r, :], wd[...])).astype(BF)
        new_rows(0, rb)

    def grad_rows(rb):
        r = slice(rb * QB, (rb + 1) * QB)
        pt[rb] = (dot_nt(dh[r, :], w1[...]) + dot_nt(pg[r, :], wqkv[...])).astype(BF)
        new_rows(1, rb)

    pieces = {
        "LN": (1.2, norm_forward), "COT": (0.9, cotangent_sum), "FF": (0.83, feed_forward),
        "FC2": (1.44, fc2_chunk), "FC1": (1.44, fc1_chunk), "QKV": (1.5, qkv_chunk), "DENSE": (1.4, dense_chunk),
        "PROJ": (1.44, project), "CG": (0.46, context_grad), "ATT": (1.09, attend), "KEY": (1.9, key_grads),
        "MIX": (0.8, mix_rows), "GRAD": (1.12, grad_rows), "BIAS": (0.23, bias_sums),
    }
    y_order += [(0 if item[0] == "MIX" else 1, item[1]) for item in ORDER if item[0] in ("MIX", "GRAD")]
    fetch(0)
    pl.semaphore_wait(barrier, len(dp_devs) + 2)
    clock.now = 4.0
    for k, item in enumerate(ORDER):
        clock.due()
        name, args = item[0], list(item[1:])
        cost, fn = pieces[name]
        if name == "GRAD":
            while not row_sums[(0, args[0])].done:
                clock.advance()
        if name == "ATT":
            cost = cost * min(args[1] + 1, 3) + 0.35
        if name == "FF":
            chained = k + 1 < len(ORDER) and ORDER[k + 1][0] == "FF"
            cost += 0.0 if ahead["ready"] else 0.3
            args.append(ORDER[k + 1][1:] if chained else None)
        if name in ("FC2", "FC1", "QKV", "DENSE"):
            args.append(KINDS[item])
        clock.now += cost
        fn(*args)
    clock.drain()
    for chunk in chunks:
        chunk.finish()
    for item in row_sums.values():
        item.finish()
    small_finish()


def fused_layer(x, g, wqkv, wd, w1, w2, seg, gain, lnb, bqkv, db, b1, b2, cos, sin):
    rows, width = x.shape
    local, ff = wd.shape[0], w1.shape[1]
    length = seg.shape[1]
    heads = local // HEAD
    nf, nrb = ff // 256, rows // 256
    nchunk = sum(len(kinds) for kinds in KINDS.values())
    any_spec, vmem = pl.BlockSpec(memory_space=pl.ANY), pl.BlockSpec(memory_space=pltpu.VMEM)

    def buf(*shape, dtype=BF):
        return pltpu.VMEM(shape, dtype)

    band = length // 2 + 256
    scratch = [
        buf(rows, width), buf(rows, width), buf(rows, ff), buf(rows, ff),
        buf(width, 3 * local), buf(local, width), buf(width, ff), buf(ff, width),
        buf(length, local), buf(length, local), buf(length, local), buf(local, length),
        buf(length, local), buf(rows, local), buf(rows, 3 * local),
        buf(local, length, dtype=F32), buf(local, length, dtype=F32),
        buf(256, band, dtype=F32), buf(16, width, dtype=F32), buf(24, width, dtype=F32),
    ]
    scratch += [buf(256, band, dtype=F32)] * 4
    scratch += [
        buf(nrb, 256, width), buf(nrb, 128, width), buf(nrb, 128, width), buf(2, 128, width),
        buf(2 * nf, 256, width), buf(3, width, local), buf(local, width),
        buf(2 * nf, 384, width), buf(3, width * 3 // 2, local), buf(local * 3 // 2, width),
        buf(width // 64, 128, dtype=F32), buf(width // 64, 128, dtype=F32),
        buf(GROUP - 1, width // 64, 128, dtype=F32),
        buf(24, 128, dtype=F32), buf(GROUP - 1, 24, 128, dtype=F32),
        pltpu.SemaphoreType.DMA((14,)), pltpu.SemaphoreType.DMA((2,)),
        pltpu.SemaphoreType.DMA((nchunk, 6)), pltpu.SemaphoreType.DMA((nchunk, 4)),
        pltpu.SemaphoreType.DMA((2 * nrb, 4)), pltpu.SemaphoreType.DMA((2 * nrb, 3)),
        pltpu.SemaphoreType.DMA((2 * GROUP,)), pltpu.SemaphoreType.DMA((2 * GROUP,)),
        pltpu.SemaphoreType.REGULAR((nrb,)),
    ]
    out_shape = [
        jax.ShapeDtypeStruct((rows, width), BF),
        jax.ShapeDtypeStruct((rows, width), BF),
        jax.ShapeDtypeStruct((ff, width), BF),
        jax.ShapeDtypeStruct((width, ff), BF),
        jax.ShapeDtypeStruct((3, width, local), BF),
        jax.ShapeDtypeStruct((local, width), BF),
        jax.ShapeDtypeStruct((width // 64, 128), F32),
        jax.ShapeDtypeStruct((24, 128), F32),
    ]
    macs = rows * width * (6 * ff + 9 * local) + 12 * heads * rows * length * HEAD
    return pl.pallas_call(
        layer_kernel,
        out_shape=out_shape,
        in_specs=[any_spec] * 6 + [vmem] * 9,
        out_specs=[any_spec] * 6 + [vmem] * 2,
        scratch_shapes=scratch,
        compiler_params=pltpu.CompilerParams(
            collective_id=0, has_side_effects=True, vmem_limit_bytes=64 * 2**20 - 2**17
        ),
        cost_estimate=pl.CostEstimate(
            flops=2 * macs, bytes_accessed=40 * 2**20, transcendentals=heads * rows * length
        ),
        name="layer",
    )(x, g, wqkv, wd, w1, w2, seg, gain, lnb, bqkv, db, b1, b2, cos, sin)


def finish_kernel(
    mixed_in, igrad_in, fc2_in, fc1_in, qkv_in, dense_in, norm_ref, bias_ref,
    mixed_out, igrad_out, gain_out, lnb_out, qkv_out, qkvb_out, dense_out, db_out, fc1_out, fc1b_out, fc2_out, b2_out,
    rows16, rows32, qkv16, qkv32, through, pass_sem, load_sem, store_sem,
):
    pieces = []
    step = rows16.shape[1]
    for src, dst in ((dense_in, dense_out), (fc2_in, fc2_out), (fc1_in, fc1_out)):
        for k in range(src.shape[0] // step):
            part, slot = pl.ds(k * step, step), len(pieces)
            pieces.append((src.at[part], dst.at[part], rows16.at[slot], rows32.at[slot]))
    for k in range(3):
        pieces.append((qkv_in.at[k], qkv_out.at[k], qkv16.at[k], qkv32.at[k]))
    loads, stores, passed = [], [], []
    for k, (src, _, low, _) in enumerate(pieces):
        loads.append(pltpu.make_async_copy(src, low, load_sem.at[k]))
        loads[-1].start()
    n = through.shape[1]
    for j, (src, dst) in enumerate(((mixed_in, mixed_out), (igrad_in, igrad_out))):
        for k in range(src.shape[0] // n):
            slot, part = len(passed), pl.ds(k * n, n)
            passed.append((
                pltpu.make_async_copy(src.at[part], through.at[slot], pass_sem.at[0, slot]),
                pltpu.make_async_copy(through.at[slot], dst.at[part], pass_sem.at[1, slot]),
            ))
            passed[-1][0].start()
    for k, (_, dst, low, wide) in enumerate(pieces):
        loads[k].wait()
        step = 32768 // low.shape[1]

        @pl.loop(0, low.shape[0] // step)
        def _(i):
            r = pl.ds(pl.multiple_of(i * step, 16), step)
            wide[r, :] = low[r, :].astype(F32)

        stores.append(pltpu.make_async_copy(wide, dst, store_sem.at[k]))
        stores[-1].start()
    for bring, take in passed:
        bring.wait()
        take.start()
    for k in range(gain_out.shape[1] // 128):
        lanes = slice(k * 128, (k + 1) * 128)
        gain_out[:, lanes] = norm_ref[k:k + 1, :]
        lnb_out[:, lanes] = norm_ref[8 + k:9 + k, :]
        fc1b_out[:, lanes] = bias_ref[k:k + 1, :]
        db_out[:, lanes] = bias_ref[16 + k:17 + k, :]
        b2_out[:, lanes] = bias_ref[16 + k:17 + k, :]
    per = qkvb_out.shape[1] // 128
    for k in range(3 * per):
        qkvb_out[k // per:k // per + 1, k % per * 128:k % per * 128 + 128] = bias_ref[8 + k:9 + k, :]
    for copy in stores + [take for _, take in passed]:
        copy.wait()


def finish(mixed, igrad, fc2, fc1, qkv, dense, norm, bias):
    width, ff, local = fc1.shape[0], fc1.shape[1], dense.shape[0]
    any_spec, vmem = pl.BlockSpec(memory_space=pl.ANY), pl.BlockSpec(memory_space=pltpu.VMEM)

    def wide(array):
        return jax.ShapeDtypeStruct(array.shape, F32)

    line = jax.ShapeDtypeStruct((1, width), F32)
    outs = [
        (mixed, any_spec), (igrad, any_spec), (line, vmem), (line, vmem), (wide(qkv), any_spec),
        (jax.ShapeDtypeStruct((3, local), F32), vmem), (wide(dense), any_spec), (line, vmem),
        (wide(fc1), any_spec), (jax.ShapeDtypeStruct((1, ff), F32), vmem), (wide(fc2), any_spec), (line, vmem),
    ]
    step = 256
    count = (dense.shape[0] + fc2.shape[0] + fc1.shape[0]) // step
    return pl.pallas_call(
        finish_kernel,
        out_shape=[jax.ShapeDtypeStruct(o.shape, o.dtype) for o, _ in outs],
        in_specs=[any_spec] * 6 + [vmem] * 2,
        out_specs=[spec for _, spec in outs],
        scratch_shapes=[
            pltpu.VMEM((count, step, width), BF), pltpu.VMEM((count, step, width), F32),
            pltpu.VMEM(qkv.shape, BF), pltpu.VMEM(qkv.shape, F32),
            pltpu.VMEM((8, mixed.shape[0] // 4, width), BF), pltpu.SemaphoreType.DMA((2, 8)),
            pltpu.SemaphoreType.DMA((count + 3,)), pltpu.SemaphoreType.DMA((count + 3,)),
        ],
        compiler_params=pltpu.CompilerParams(vmem_limit_bytes=56 * 2**20),
        cost_estimate=pl.CostEstimate(flops=0, bytes_accessed=36 * 2**20, transcendentals=0),
        name="finish",
    )(mixed, igrad, fc2, fc1, qkv, dense, norm, bias)


def local_part(
    n_dp, tokens, segment_ids, ln_gain, ln_bias, qkv_weight, qkv_bias, dense_weight, dense_bias,
    fc1_weight, fc1_bias, fc2_weight, fc2_bias, cotangent,
):
    width = tokens.shape[1]
    local = qkv_weight.shape[2]
    cos, sin = rotary_tables(segment_ids.shape[1])
    outs = fused_layer(
        tokens, cotangent, qkv_weight.transpose(1, 0, 2), dense_weight, fc1_weight, fc2_weight,
        segment_ids, ln_gain[None], ln_bias[None], qkv_bias, dense_bias[None],
        fc1_bias[None], fc2_bias[None], cos, sin,
    )
    mixed, igrad, sums = outs[0], outs[1], list(outs[2:])
    if n_dp > GROUP:
        groups = [[k + GROUP * j for j in range(n_dp // GROUP)] for k in range(GROUP)]
        sums = [lax.psum(s, "dp", axis_index_groups=groups) for s in sums]
    done = finish(mixed, igrad, *sums)
    mixed, igrad, gain, lnb, qkv, qkvb, dense, db, fc1, b1, fc2, b2 = done
    return (
        mixed, igrad, gain.reshape(width), lnb.reshape(width), qkv.transpose(1, 0, 2), qkvb, dense,
        db.reshape(width), fc1, b1.reshape(fc1_bias.shape), fc2, b2.reshape(width),
    )


def solution(mesh):
    row, whole = P("dp", None), P()
    weights = (
        whole, whole, P(None, None, "tensor"), P(None, "tensor"), P("tensor", None), whole,
        P(None, "tensor"), P("tensor"), P("tensor", None), whole,
    )
    return jax.shard_map(
        functools.partial(local_part, mesh.shape["dp"]),
        mesh=mesh,
        in_specs=(row, row) + weights + (row,),
        out_specs=(row, row) + weights,
        check_vma=False,
    )
```

```python
import functools
import heapq

import jax
import jax.numpy as jnp
import numpy as np
from jax import lax
from jax.experimental import pallas as pl
from jax.experimental.pallas import tpu as pltpu
from jax.sharding import PartitionSpec as P

HEAD = 64
ROTARY = 32
NORM_EPS = 1e-05
MASKED = -1e30
BASE = 10000.0
BF = jnp.bfloat16
F32 = jnp.float32
MESH = pl.DeviceIdType.MESH
GROUP = 8

ORDER = (
    ("LN", 0), ("FF", 3, 0), ("LN", 1), ("LN", 2), ("LN", 3), ("PROJ", 0, 0), ("FF", 0, 2), ("FF", 3, 2),
    ("FF", 0, 3), ("FF", 3, 1), ("FF", 3, 3), ("FF", 0, 0), ("FF", 0, 1), ("FF", 1, 0), ("FC2", 0), ("FC2", 3),
    ("CG", 0, 0), ("FF", 2, 2), ("FF", 1, 1), ("FF", 2, 3), ("FF", 2, 0), ("FF", 1, 3), ("FF", 2, 1), ("FF", 1, 2),
    ("ATT", 0, 1), ("FC1", 2), ("MIX", 1), ("PROJ", 0, 1), ("CG", 0, 1), ("FC1", 3), ("ATT", 0, 0), ("MIX", 0),
    ("ATT", 0, 2), ("MIX", 2), ("FC2", 2), ("ATT", 0, 3), ("MIX", 3), ("KEY", 0), ("FC1", 1), ("GRAD", 1),
    ("CG", 1, 0), ("PROJ", 1, 0), ("ATT", 1, 1), ("MIX", 5), ("FC2", 1), ("ATT", 1, 0), ("MIX", 4), ("GRAD", 2),
    ("FC1", 0), ("PROJ", 1, 1), ("CG", 1, 1), ("ATT", 1, 3), ("MIX", 7), ("ATT", 1, 2), ("GRAD", 3), ("DENSE",),
    ("MIX", 6), ("KEY", 1), ("QKV", 1), ("QKV", 2), ("GRAD", 0), ("QKV", 0), ("GRAD", 4), ("GRAD", 5), ("GRAD", 6),
    ("GRAD", 7), ("BIAS",),
)
KINDS = {
    ("FC2", 0): "AB", ("FC2", 1): "AB", ("FC2", 2): "BA", ("FC2", 3): "BA", ("FC1", 0): "AA", ("FC1", 1): "AB",
    ("FC1", 2): "BA", ("FC1", 3): "AA", ("QKV", 0): "AA", ("QKV", 1): "AA", ("QKV", 2): "AB", ("DENSE",): "AA",
}


def dot(a, b):
    return lax.dot_general(a, b, (((1,), (0,)), ((), ())), preferred_element_type=F32)


def dot_nt(a, b):
    return lax.dot_general(a, b, (((1,), (1,)), ((), ())), preferred_element_type=F32)


def dot_tn(a, b):
    return lax.dot_general(a, b, (((0,), (0,)), ((), ())), preferred_element_type=F32)


def rotary_tables(length):
    half = ROTARY // 2
    frequency = (BASE ** (-(np.arange(half, dtype=np.float32) * 2.0) / ROTARY)).astype(np.float32)
    angles = np.arange(length, dtype=np.float32)[:, None] * frequency[None, :]
    cosine, sine = np.cos(angles), np.sin(angles)
    rest = HEAD - ROTARY
    c = np.concatenate([cosine, cosine, np.ones((length, rest), np.float32)], axis=1)
    s = np.concatenate([-sine, sine, np.zeros((length, rest), np.float32)], axis=1)
    return np.tile(c, (1, 2)).astype(np.float32), np.tile(s, (1, 2)).astype(np.float32)


def pair_swap(u):
    lane = lax.broadcasted_iota(jnp.int32, u.shape, 1)
    half = ROTARY // 2
    return jnp.where(lane % ROTARY < half, pltpu.roll(u, 128 - half, 1), pltpu.roll(u, half, 1))


class Clock:
    UNIT_KIB = 128
    UNIT_US = 2.85
    CORE_US = 0.4
    LATENCY = 2.8
    MARGIN = 0.5
    STEP_US = 0.12
    ADD_US = 0.03

    def __init__(self):
        self.now = 0.0
        self.queue = []
        self.count = 0
        self.free = {}

    def at(self, when, step):
        heapq.heappush(self.queue, (when, self.count, step))
        self.count += 1

    def arrival(self, link, units):
        start = max(self.now, self.free.get(link, 0.0))
        self.free[link] = start + units * (self.CORE_US if link == "core" else self.UNIT_US)
        return self.free[link] + self.LATENCY + self.MARGIN

    def spend(self, adds=0.0, more=0.0):
        self.now += self.STEP_US + self.ADD_US * adds + more

    def advance(self):
        when, _, step = heapq.heappop(self.queue)
        self.now = max(self.now, when)
        step()

    def due(self):
        while self.queue and self.queue[0][0] <= self.now:
            self.advance()

    def drain(self):
        while self.queue:
            self.advance()


def layer_kernel(
    x_hbm, g_hbm, wqkv_hbm, wd_hbm, w1_hbm, w2_hbm,
    seg_ref, gain_ref, lnb_ref, bqkv_ref, db_ref, b1_ref, b2_ref, cos_ref, sin_ref,
    mixed_hbm, igrad_hbm, fc2_hbm, fc1_hbm, qkv_hbm, dense_hbm, norm_out, bias_out,
    nb, gb, act, dh, wqkv, wd, w1, w2,
    qs, ks, vs, qT, cg, ctx, pg, dkT, dvT, bias, gacc,
    s0, s1, d0, d1,
    pt, t1r, t2r, xs, gA, gQ, gD, rA, rQ, rD,
    norm_send, norm_core, norm_recv, bias_send, bias_recv,
    load_sem, x_sem, dp_send, dp_recv, t_send, t_recv, sm_send, sm_recv, credit,
):
    rows, width = nb.shape
    seqs, length = seg_ref.shape
    local = wd.shape[0]
    ff = w1.shape[1]
    heads = local // HEAD
    QB = 256
    nrb = rows // QB
    HB = QB // 2

    dp, tensor = lax.axis_index("dp"), lax.axis_index("tensor")
    base = dp - lax.rem(dp, GROUP)
    me = lax.rem(dp, GROUP)
    xx, zz = lax.rem(me, 2), me // 2
    yy, cc = tensor // 2, lax.rem(tensor, 2)
    x_dev = (base + zz * 2 + (1 - xx), tensor)
    pair_dev = (base + (zz + 1 - 2 * lax.rem(zz, 2)) * 2 + xx, tensor)
    mid_dev = (base + (3 - zz) * 2 + xx, tensor)
    y_dev = (dp, (1 - yy) * 2 + cc)
    c_dev = (dp, yy * 2 + (1 - cc))
    side = zz // 2
    inner = (zz == 1) | (zz == 2)
    outer = jnp.logical_not(inner)
    dp_devs = [(base + lax.rem(me + k, GROUP), tensor) for k in range(1, GROUP)]

    barrier = pltpu.get_barrier_semaphore()
    for device in dp_devs + [y_dev, c_dev]:
        pl.semaphore_signal(barrier, inc=1, device_id=device, device_id_type=MESH)

    loads = {}

    def load(name, src, dst):
        loads[name] = pltpu.make_async_copy(src, dst, load_sem.at[len(loads)])
        loads[name].start()

    quarter = rows // 4
    parts = [pl.ds(k * quarter, quarter) for k in range(4)]
    load("x0", x_hbm.at[parts[0]], act.at[parts[0]])
    load("w1", w1_hbm, w1)
    load("w2", w2_hbm, w2)
    load("g0", g_hbm.at[parts[0]], gb.at[parts[0]])
    for k in range(1, 4):
        load(f"x{k}", x_hbm.at[parts[k]], act.at[parts[k]])
        load(f"g{k}", g_hbm.at[parts[k]], gb.at[parts[k]])
    for k in range(3):
        load(f"wqkv{k}", wqkv_hbm.at[k], wqkv.at[:, k * local:(k + 1) * local])
    load("wd", wd_hbm, wd)
    gacc[...] = jnp.zeros_like(gacc)

    clock = Clock()
    cgT = gD.at[:, pl.ds(0, length)]
    prob_low = [[gQ.at[j, pl.ds(k * QB, QB)] for j in range(3)] for k in range(4)]

    def remote(src, dst, send_sem, recv_sem, device):
        return pltpu.make_async_remote_copy(
            src_ref=src, dst_ref=dst, send_sem=send_sem, recv_sem=recv_sem,
            device_id=device, device_id_type=MESH,
        )

    def span(first, n):
        return pl.ds(pl.multiple_of(first, 16), n)

    def add_rows(dst, a_ref, b_ref):
        n, cols = dst.shape
        step = min(n, 131072 // cols)
        if n % step:
            step = 48

        if n == step:
            dst[...] = a_ref[...] + b_ref[...]
            return

        @pl.loop(0, n // step)
        def _(k):
            r = span(k * step, step)
            dst[r, :] = a_ref[r, :] + b_ref[r, :]

    class PairFirst:
        def __init__(self, k, own, got, out, out_row):
            h = own.shape[0] // 2
            self.h, self.units = h, h * own.shape[1] * 2 / 1024 / clock.UNIT_KIB
            self.xr, self.zi, self.zm = (got.at[pl.ds(j * h, h)] for j in range(3))
            self.keep = own.at[span(xx * h, h)]
            target = out.at[span(out_row + xx * h, h)]
            send, recv = dp_send.at[k], dp_recv.at[k]
            self.c_x = remote(own.at[span((1 - xx) * h, h)], self.xr, send.at[0], recv.at[0], x_dev)
            self.c_in = remote(self.xr, self.zi, send.at[1], recv.at[1], pair_dev)
            self.c_mid = remote(self.zi, self.zm, send.at[2], recv.at[2], mid_dev)
            self.c_out = remote(self.zm, self.zm, send.at[1], recv.at[2], pair_dev)
            self.c_ag = remote(self.zm, target, send.at[3], recv.at[3], x_dev)
            self.c_loc = pltpu.make_async_copy(self.zm, target, send.at[4])

        def start(self):
            self.c_x.start()
            clock.spend()
            clock.at(clock.arrival("x", self.units), self.pair_sum)

        def pair_sum(self):
            self.c_x.wait_recv()
            add_rows(self.xr, self.xr, self.keep)

            @pl.when(outer)
            def _():
                self.c_in.start()

            clock.spend(self.units)
            clock.at(clock.arrival("zin", self.units), self.side_sum)

        def side_sum(self):
            @pl.when(inner)
            def _():
                self.c_in.wait_recv()
                add_rows(self.zi, self.zi, self.xr)
                self.c_mid.start()

            clock.spend(self.units)
            clock.at(clock.arrival("zmid", self.units), self.line_sum)

        def line_sum(self):
            @pl.when(inner)
            def _():
                self.c_mid.wait_recv()
                self.c_mid.wait_send()
                add_rows(self.zm, self.zm, self.zi)
                self.c_out.start()
                self.c_ag.start()
                self.c_loc.start()

            clock.spend(self.units)
            clock.at(clock.arrival("zout", self.units), self.outer_end)

        def outer_end(self):
            @pl.when(outer)
            def _():
                self.c_mid.wait_recv()
                self.c_ag.start()
                self.c_loc.start()

            clock.spend()
            clock.arrival("x", self.units)

        def finish(self):
            self.c_x.wait_send()
            self.c_in.wait_send()
            self.c_ag.wait()
            self.c_loc.wait()

    class LineFirst:
        def __init__(self, k, own, got, out, out_row):
            n = own.shape[0]
            b = n // 4
            self.b, self.units = b, b * own.shape[1] * 2 / 1024 / clock.UNIT_KIB
            self.r1, self.r2, self.xb = got.at[pl.ds(0, 3 * b)], got.at[pl.ds(3 * b, 2 * b)], got.at[pl.ds(5 * b, b)]
            rest = own.at[span((1 - side) * b, 3 * b)]
            self.mine = own.at[span(zz * b, b)]
            self.far = own.at[span((1 - side) * 2 * b, 2 * b)]
            near = own.at[span(side * 2 * b, 2 * b)]
            self.outers = own.at[span(side * 3 * b, b)]
            self.r1_far = self.r1.at[span((1 - side) * b, 2 * b)]
            self.r1_mine = self.r1.at[span(side * 2 * b, b)]
            self.r2_mine = self.r2.at[span((1 - side) * b, b)]
            self.r2_outer = self.r2.at[span(side * b, b)]
            r1_first = self.r1.at[pl.ds(0, b)]
            self.r1_first = r1_first
            send, recv = dp_send.at[k], dp_recv.at[k]
            self.c_1 = remote(rest, self.r1, send.at[0], recv.at[0], pair_dev)
            self.c_2 = remote(self.r1_far, self.r2, send.at[0], recv.at[1], mid_dev)
            self.c_3 = remote(self.r2_outer, r1_first, send.at[1], recv.at[0], pair_dev)
            self.c_x = remote(self.mine, self.xb, send.at[2], recv.at[2], x_dev)
            self.c_5 = remote(self.mine, self.mine, send.at[1], recv.at[3], pair_dev)
            self.c_5r = remote(self.outers, self.outers, send.at[1], recv.at[3], pair_dev)
            self.c_6 = remote(near, near, send.at[3], recv.at[1], mid_dev)
            self.c_6r = remote(self.far, self.far, send.at[3], recv.at[1], mid_dev)
            self.c_7 = remote(rest, rest, send.at[4], recv.at[3], pair_dev)
            self.c_loc = pltpu.make_async_copy(own, out.at[span(out_row, n)], send.at[5])

        def start(self):
            @pl.when(outer)
            def _():
                self.c_1.start()

            clock.spend(2 * self.units)
            clock.at(clock.arrival("zin", 3 * self.units), self.side_sum)

        def side_sum(self):
            @pl.when(inner)
            def _():
                self.c_1.wait_recv()
                add_rows(self.r1_far, self.r1_far, self.far)
                self.c_2.start()
                add_rows(self.r1_mine, self.r1_mine, self.mine)

            clock.spend(2 * self.units)
            clock.at(clock.arrival("zmid", 2 * self.units), self.line_sum)

        def line_sum(self):
            @pl.when(inner)
            def _():
                self.c_2.wait_recv()
                add_rows(self.r2_outer, self.r2_outer, self.outers)
                self.c_3.start()
                add_rows(self.mine, self.r1_mine, self.r2_mine)
                self.c_x.start()

            clock.spend(2 * self.units)
            clock.at(clock.arrival("zout", self.units), self.outer_sum)

        def outer_sum(self):
            @pl.when(outer)
            def _():
                self.c_3.wait_recv()
                add_rows(self.mine, self.mine, self.r1_first)
                self.c_x.start()

            clock.spend(2 * self.units)
            clock.at(clock.arrival("x", self.units), self.pair_sum)

        def pair_sum(self):
            self.c_x.wait()
            add_rows(self.mine, self.mine, self.xb)

            @pl.when(outer)
            def _():
                self.c_1.wait_send()
                self.c_5.start()

            clock.spend(2 * self.units)
            clock.at(clock.arrival("zin", self.units), self.side_gather)

        def side_gather(self):
            @pl.when(inner)
            def _():
                self.c_5r.wait_recv()
                self.c_6.start()

            clock.spend(2 * self.units)
            clock.at(clock.arrival("zmid", 2 * self.units), self.line_gather)

        def line_gather(self):
            @pl.when(inner)
            def _():
                self.c_6r.wait_recv()
                self.c_7.start()
                self.c_loc.start()

            clock.spend(2 * self.units)
            clock.at(clock.arrival("zout", 3 * self.units), self.outer_end)

        def outer_end(self):
            @pl.when(outer)
            def _():
                self.c_7.wait_recv()
                self.c_loc.start()

        def finish(self):
            @pl.when(outer)
            def _():
                self.c_5.wait_send()

            @pl.when(inner)
            def _():
                self.c_2.wait_send()
                self.c_3.wait_send()
                self.c_6.wait_send()
                self.c_7.wait_send()

            self.c_loc.wait()

    chunks = []

    kind_of = {"A": PairFirst, "B": LineFirst}

    waited = []

    def entered():
        if not waited:
            pl.semaphore_wait(barrier, len(dp_devs) + 2)
            waited.append(True)

    def new_chunk(own, got, out, out_row, kinds):
        entered()
        n, m = own.shape[0] // len(kinds), got.shape[0] // len(kinds)
        for k, kind in enumerate(kinds):
            part = own.at[pl.ds(k * n, n)]
            chunk = kind_of[kind](len(chunks), part, got.at[pl.ds(k * m, m)], out, out_row + k * n)
            chunks.append(chunk)
            chunk.start()

    y_order = []
    mine = span(cc * HB, HB)
    other = span((1 - cc) * HB, HB)

    def fetch(seq):
        if seq < len(y_order):
            rb = y_order[seq][1]
            src = x_hbm.at[span(rb * QB + cc * HB, HB)]
            pltpu.make_async_copy(src, xs.at[seq % 2], x_sem.at[seq % 2]).start()

    def row_stats(x):
        mu = jnp.mean(x, axis=1, keepdims=True)
        cent = x - mu
        rstd = lax.rsqrt(jnp.mean(cent * cent, axis=1, keepdims=True) + NORM_EPS)
        return cent * rstd, rstd

    class RowSum:
        def __init__(self, phase, rb):
            self.phase, self.rb, self.done = phase, rb, False
            k = phase * nrb + rb
            out = igrad_hbm if phase else mixed_hbm
            target = out.at[span(rb * QB + cc * HB, HB)]
            self.own = own = pt.at[rb, mine]
            self.units = HB * width * 2 / 1024 / clock.UNIT_KIB
            send, recv = t_send.at[k], t_recv.at[k]
            self.c_core = remote(pt.at[rb, other], t1r.at[rb], send.at[0], recv.at[0], c_dev)
            self.c_y = remote(own, t2r.at[rb], send.at[1], recv.at[1], y_dev)
            self.c_fin = remote(t2r.at[rb], target, send.at[2], recv.at[2], c_dev)
            self.c_loc = pltpu.make_async_copy(t2r.at[rb], target, send.at[3])

        def start(self):
            if self.phase:
                before = row_sums[(0, self.rb)]
                before.c_fin.wait_recv()
            self.c_core.start()
            clock.spend()
            clock.at(clock.arrival("core", self.units), self.chip_sum)

        def chip_sum(self):
            self.c_core.wait_recv()
            add_rows(self.own, self.own, t1r.at[self.rb])
            if self.phase:
                pl.semaphore_wait(credit.at[self.rb], 1)
            self.c_y.start()
            clock.spend(self.units)
            clock.at(clock.arrival("y", self.units), self.whole_sum)

        def whole_sum(self):
            rb = self.rb
            seq = y_order.index((self.phase, rb))
            slot = seq % 2
            fetch(seq + 1)
            pltpu.make_async_copy(x_hbm.at[pl.ds(0, HB)], xs.at[slot], x_sem.at[slot]).wait()
            self.c_y.wait_recv()
            step = 16
            own, arrived = self.own, t2r.at[rb]
            gsum, bsum = gacc[0:8, :], gacc[8:16, :]
            for j in range(HB // step):
                first = j * step
                r = pl.ds(first, step)
                x = xs[slot, r, :].astype(F32)
                total = own[r, :].astype(F32) + arrived[r, :].astype(F32)
                if self.phase == 0:
                    arrived[r, :] = (x + total + (db_ref[...] + b2_ref[...])).astype(BF)
                else:
                    xhat, rstd = row_stats(x)
                    gsum += jnp.sum((total * xhat).reshape(step // 8, 8, width), axis=0)
                    bsum += jnp.sum(total.reshape(step // 8, 8, width), axis=0)
                    e = total * gain_ref[...]
                    m1 = jnp.mean(e, axis=1, keepdims=True)
                    m2 = jnp.mean(e * xhat, axis=1, keepdims=True)
                    gr = span(rb * QB + cc * HB + first, step)
                    grad = gb[gr, :].astype(F32) + rstd * (e - m1 - xhat * m2)
                    arrived[r, :] = grad.astype(BF)
            if self.phase:
                gacc[0:8, :], gacc[8:16, :] = gsum, bsum
            self.c_fin.start()
            self.c_loc.start()
            clock.spend(0, 0.5 if self.phase else 0.3)
            if self.phase == 0:
                clock.at(clock.now + 4.0, self.give_back)
            elif seq == len(y_order) - 1:
                clock.at(clock.now, norm_sums)

        def give_back(self):
            clock.spend()
            self.c_fin.wait_send()
            self.c_loc.wait()
            self.c_core.wait_send()
            self.c_y.wait_send()
            pl.semaphore_signal(credit.at[self.rb], inc=1, device_id=y_dev, device_id_type=MESH)
            self.done = True

        def finish(self):
            if self.phase:
                self.c_core.wait_send()
                self.c_y.wait_send()
                self.c_fin.wait()
                self.c_loc.wait()

    row_sums = {}

    def new_rows(phase, rb):
        entered()
        row_sums[(phase, rb)] = RowSum(phase, rb)
        row_sums[(phase, rb)].start()

    small = []

    def fold(dst, first, line):
        for k in range(line.shape[1] // 128):
            dst[first + k:first + k + 1, :] = line[:, k * 128:(k + 1) * 128]

    def send_small(src, slots, first_sem):
        for k, device in enumerate(dp_devs):
            sem = first_sem + k
            copy = remote(src, slots.at[k], sm_send.at[sem], sm_recv.at[sem], device)
            copy.start()
            small.append(copy)

    def sum_small(src, slots):
        total = jnp.zeros(src.shape, F32)
        for place in range(GROUP):
            behind = lax.rem(me - place + GROUP, GROUP)
            there = slots[jnp.maximum(behind - 1, 0)]
            total = total + jnp.where(behind == 0, src[...], there)
        return total

    def bias_sums():
        ones = jnp.ones((16, rows), BF)
        bias_send[...] = jnp.zeros_like(bias_send)
        for k, array in enumerate((dh, pg, gb)):
            fold(bias_send, 8 * k, dot(ones, array[...])[0:1, :])
        send_small(bias_send, bias_recv, 1)

    def norm_sums():
        for k in range(2):
            fold(norm_send, 8 * k, jnp.sum(gacc[8 * k:8 * k + 8, :], axis=0, keepdims=True))
        swap = remote(norm_send, norm_core, sm_send.at[0], sm_recv.at[0], c_dev)
        swap.start()
        swap.wait()
        norm_send[...] = norm_send[...] + norm_core[...]
        send_small(norm_send, norm_recv, GROUP)

    def small_finish():
        for copy in small:
            copy.wait()
        norm_out[...] = sum_small(norm_send, norm_recv)
        bias_out[...] = sum_small(bias_send, bias_recv)

    def wait_load(*names):
        for name in names:
            if name in loads:
                loads.pop(name).wait()

    def norm_forward(k):
        step = 16
        wait_load(f"x{k}")
        for j in range(quarter // step):
            r = slice(k * quarter + j * step, k * quarter + (j + 1) * step)
            xhat, _ = row_stats(act[r, :].astype(F32))
            nb[r, :] = (xhat * gain_ref[...] + lnb_ref[...]).astype(BF)

    def ff_products(j, q, slot):
        wait_load("w1", "w2", f"g{q}")
        cols, r = slice(j * 256, (j + 1) * 256), slice(q * quarter, (q + 1) * quarter)
        h = dot(nb[r, :], w1[:, cols])
        up = dot_nt(gb[r, :], w2[cols, :])
        for k in range(quarter // 256):
            (s0, s1)[slot][:, k * 256:(k + 1) * 256] = h[k * 256:(k + 1) * 256]
            (d0, d1)[slot][:, k * 256:(k + 1) * 256] = up[k * 256:(k + 1) * 256]

    def ff_gelu(j, q, slot):
        cols = slice(j * 256, (j + 1) * 256)
        step = 32
        k0 = 0.7978845608028654
        for t in range(quarter // step):
            at = slice(t * step % 256, t * step % 256 + step)
            lane = slice(t * step // 256 * 256, t * step // 256 * 256 + 256)
            r = slice(q * quarter + t * step, q * quarter + (t + 1) * step)
            h = (s0, s1)[slot][at, lane] + b1_ref[:, cols]
            up = (d0, d1)[slot][at, lane]
            h2 = h * h
            th = jnp.tanh(k0 * h * (1.0 + 0.044715 * h2))
            half = 0.5 * (1.0 + th)
            act[r, cols] = (h * half).astype(BF)
            slope = half + 0.5 * h * (1.0 - th * th) * (k0 * (1.0 + 3 * 0.044715 * h2))
            hg = (up * slope).astype(BF)
            dh[r, cols] = hg

    ahead = {"slot": 0, "ready": False}

    def feed_forward(j, q, following=None):
        slot = ahead["slot"]
        if not ahead["ready"]:
            ff_products(j, q, slot)
        if following:
            ff_products(*following, 1 - slot)
        ahead["slot"], ahead["ready"] = 1 - slot, bool(following)
        ff_gelu(j, q, slot)

    nf = ff // 256

    def fc2_chunk(j, kind):
        wait_load("g0", "g1", "g2", "g3")
        gA[j] = dot_tn(act[:, j * 256:(j + 1) * 256], gb[...]).astype(BF)
        new_chunk(gA.at[j], rA.at[j], fc2_hbm, j * 256, kind)

    def fc1_chunk(j, kind):
        k = nf + j
        gA[k] = dot_tn(nb[:, j * 256:(j + 1) * 256], dh[...]).astype(BF)
        new_chunk(gA.at[k], rA.at[k], fc1_hbm, j * 256, kind)

    def qkv_chunk(j, kind):
        for k in range(2):
            at = slice(k * width // 2, (k + 1) * width // 2)
            gQ[j, at, :] = dot_tn(nb[:, at], pg[:, j * local:(j + 1) * local]).astype(BF)
        new_chunk(gQ.at[j], rQ.at[j], qkv_hbm.at[j], 0, kind)

    def dense_chunk(kind):
        gD[...] = dot_tn(ctx[...], gb[...]).astype(BF)
        new_chunk(gD, rD, dense_hbm, 0, kind)

    def project(s, half):
        wait_load("wqkv0", "wqkv1", "wqkv2")
        for i in range(half * length // 512, (half + 1) * length // 512):
            r = slice(i * 256, (i + 1) * 256)
            src = slice(s * length + i * 256, s * length + (i + 1) * 256)
            c, sn = cos_ref[r, :], sin_ref[r, :]
            whole = dot(nb[src, :], wqkv[...])
            for part in range(3):
                y = whole[:, part * local:(part + 1) * local] + bqkv_ref[part:part + 1, :]
                for pr in range(heads // 2):
                    lanes = slice(pr * 128, (pr + 1) * 128)
                    u = y[:, lanes]
                    if part < 2:
                        u = u * c + pair_swap(u) * sn
                    if part == 0:
                        u = u * (HEAD ** -0.5)
                        qT[lanes, r] = u.T.astype(BF)
                    (qs, ks, vs)[part][r, lanes] = u.astype(BF)

    def context_grad(s, half):
        wait_load("wd", f"g{2 * s + half}")
        r = slice(half * length // 2, (half + 1) * length // 2)
        u = dot_nt(gb[s * length + half * length // 2:s * length + (half + 1) * length // 2, :], wd[...])
        cg[r, :] = u.astype(BF)
        cgT[:, r] = u.T.astype(BF)

    touched = set()

    def attend(s, i):
        blocks = length // QB
        lo = max(0, i - blocks // 2)
        n = (i + 1 - lo) * QB
        qrows = slice(i * QB, (i + 1) * QB)
        keys = slice(lo * QB, (i + 1) * QB)
        at_rows = slice(s * length + i * QB, s * length + (i + 1) * QB)
        seg = seg_ref[s:s + 1, :].astype(F32)
        qseg = jnp.broadcast_to(seg[:, qrows], (128, QB)).T
        for t in range(n // 128):
            at = lo * QB + t * 128
            kseg = jnp.broadcast_to(seg[:, at:at + 128], (QB, 128))
            qpos = i * QB + lax.broadcasted_iota(jnp.int32, (QB, 128), 0)
            kpos = at + lax.broadcasted_iota(jnp.int32, (QB, 128), 1)
            ok = (kpos <= qpos) & (kseg == qseg)
            bias[:, t * 128:(t + 1) * 128] = jnp.where(ok, 0.0, MASKED)
        low = lax.broadcasted_iota(jnp.int32, (QB, 128), 1) < HEAD
        zero = jnp.zeros((), BF)

        def head_of(u, h):
            return jnp.where(low, u, zero) if h % 2 == 0 else jnp.where(low, zero, u)

        def scores(h):
            lanes = slice(h // 2 * 128, h // 2 * 128 + 128)
            (s0, s1)[h % 2][:, :n] = dot_nt(head_of(qs[qrows, lanes], h), ks[keys, lanes])
            (d0, d1)[h % 2][:, :n] = dot_nt(head_of(cg[qrows, lanes], h), vs[keys, lanes])

        def soft(h):
            step = 16
            sc_ref, dp_ref = (s0, s1)[h % 2], (d0, d1)[h % 2]

            def put(dst, r, first, value):
                for j in range(first // HB, first // HB + value.shape[1] // HB):
                    dst[j // 2][r, j % 2 * HB:(j % 2 + 1) * HB] = value[:, j * HB - first:(j + 1) * HB - first]

            for t in range(QB // step):
                r = slice(t * step, (t + 1) * step)
                top = i * QB + t * step // HB * HB
                first, last = max(0, top - length // 2) - lo * QB, top + HB - lo * QB
                first = max(0, first)
                if h < 2:
                    for gap, wide in ((0, first), (last, n - last)):
                        if wide:
                            for dst in (prob_low[h % 2], prob_low[2 + h % 2]):
                                put(dst, r, gap, jnp.zeros((step, wide), BF))
                sc = sc_ref[r, first:last] + bias[r, first:last]
                e = jnp.exp(sc - jnp.max(sc, axis=1, keepdims=True))
                p = e * (1.0 / jnp.sum(e, axis=1, keepdims=True))
                put(prob_low[h % 2], r, first, p.astype(BF))
                pd = p * dp_ref[r, first:last]
                delta = jnp.sum(pd, axis=1, keepdims=True)
                put(prob_low[2 + h % 2], r, first, (pd - p * delta).astype(BF))

        def products(h, kept):
            lanes = slice(h // 2 * 128, h // 2 * 128 + 128)
            hr = slice(h * HEAD, (h + 1) * HEAD)
            p, e = (jnp.concatenate([prob_low[k][j][...] for j in range(n // QB)], axis=1) for k in (h % 2, 2 + h % 2))
            kept.append((dot(p, vs[keys, lanes]), dot(e, ks[keys, lanes])))
            for total, new in ((dvT, dot(cgT[hr, qrows], p)), (dkT, dot(qT[hr, qrows], e))):
                for j in range(n // QB):
                    at = slice((lo + j) * QB, (lo + j + 1) * QB)
                    part = new[:, j * QB:(j + 1) * QB]
                    total[hr, at] = total[hr, at] + part if (s, lo + j) in touched else part
            if h % 2:
                (o_a, q_a), (o_b, q_b) = kept
                kept.clear()
                ctx[at_rows, lanes] = jnp.where(low, o_a, o_b).astype(BF)
                u = jnp.where(low, q_a, q_b) * (HEAD ** -0.5)
                u = u * cos_ref[qrows, :] - pair_swap(u) * sin_ref[qrows, :]
                pg[at_rows, lanes] = u.astype(BF)

        kept = []
        scores(0)
        for h in range(heads):
            if h + 1 < heads:
                scores(h + 1)
            soft(h)
            products(h, kept)
        touched.update((s, lo + j) for j in range(n // QB))

    def key_grads(s):
        for i in range(length // 256):
            r = slice(i * 256, (i + 1) * 256)
            dst = slice(s * length + i * 256, s * length + (i + 1) * 256)
            c, sn = cos_ref[r, :], sin_ref[r, :]
            for pr in range(heads // 2):
                u = dkT[pr * 128:(pr + 1) * 128, r].T
                u = u * c - pair_swap(u) * sn
                pg[dst, local + pr * 128:local + (pr + 1) * 128] = u.astype(BF)
                u = dvT[pr * 128:(pr + 1) * 128, r].T
                pg[dst, 2 * local + pr * 128:2 * local + (pr + 1) * 128] = u.astype(BF)


    def mix_rows(rb):
        r = slice(rb * QB, (rb + 1) * QB)
        pt[rb] = (dot(act[r, :], w2[...]) + dot(ctx[r, :], wd[...])).astype(BF)
        new_rows(0, rb)

    def grad_rows(rb):
        r = slice(rb * QB, (rb + 1) * QB)
        pt[rb] = (dot_nt(dh[r, :], w1[...]) + dot_nt(pg[r, :], wqkv[...])).astype(BF)
        new_rows(1, rb)

    pieces = {
        "LN": (0.79, norm_forward), "FF": (0.63, feed_forward),
        "FC2": (1.31, fc2_chunk), "FC1": (1.31, fc1_chunk), "QKV": (1.26, qkv_chunk), "DENSE": (1.26, dense_chunk),
        "PROJ": (1.1, project), "CG": (0.42, context_grad), "ATT": (0.89, attend), "KEY": (1.37, key_grads),
        "MIX": (0.74, mix_rows), "GRAD": (1.02, grad_rows), "BIAS": (1.26, bias_sums),
    }
    y_order += [(0 if item[0] == "MIX" else 1, item[1]) for item in ORDER if item[0] in ("MIX", "GRAD")]
    fetch(0)
    clock.now = 4.0
    run = 0
    for k, item in enumerate(ORDER):
        run = run + 1 if k and item[0] == ORDER[k - 1][0] == "FF" else 0
        if run % 6 == 0:
            clock.due()
        name, args = item[0], list(item[1:])
        cost, fn = pieces[name]
        if name == "GRAD":
            while not row_sums[(0, args[0])].done:
                clock.advance()
        if name == "ATT":
            cost = cost * min(args[1] + 1, 3) + 0.26
        if name == "FF":
            chained = k + 1 < len(ORDER) and ORDER[k + 1][0] == "FF"
            cost += 0.0 if ahead["ready"] else 0.37
            args.append(ORDER[k + 1][1:] if chained else None)
        if name in ("FC2", "FC1", "QKV", "DENSE"):
            args.append(KINDS[item])
        clock.now += cost
        fn(*args)
    clock.drain()
    for chunk in chunks:
        chunk.finish()
    for item in row_sums.values():
        item.finish()
    small_finish()


def fused_layer(x, g, wqkv, wd, w1, w2, seg, gain, lnb, bqkv, db, b1, b2, cos, sin):
    rows, width = x.shape
    local, ff = wd.shape[0], w1.shape[1]
    length = seg.shape[1]
    heads = local // HEAD
    nf, nrb = ff // 256, rows // 256
    nchunk = sum(len(kinds) for kinds in KINDS.values())
    any_spec, vmem = pl.BlockSpec(memory_space=pl.ANY), pl.BlockSpec(memory_space=pltpu.VMEM)

    def buf(*shape, dtype=BF):
        return pltpu.VMEM(shape, dtype)

    band = length // 2 + 256
    scratch = [
        buf(rows, width), buf(rows, width), buf(rows, ff), buf(rows, ff),
        buf(width, 3 * local), buf(local, width), buf(width, ff), buf(ff, width),
        buf(length, local), buf(length, local), buf(length, local), buf(local, length),
        buf(length, local), buf(rows, local), buf(rows, 3 * local),
        buf(local, length, dtype=F32), buf(local, length, dtype=F32),
        buf(256, band, dtype=F32), buf(16, width, dtype=F32),
    ]
    scratch += [buf(256, band, dtype=F32)] * 4
    scratch += [
        buf(nrb, 256, width), buf(nrb, 128, width), buf(nrb, 128, width), buf(2, 128, width),
        buf(2 * nf, 256, width), buf(3, width, local), buf(local, width),
        buf(2 * nf, 384, width), buf(3, width * 3 // 2, local), buf(local * 3 // 2, width),
        buf(width // 64, 128, dtype=F32), buf(width // 64, 128, dtype=F32),
        buf(GROUP - 1, width // 64, 128, dtype=F32),
        buf(24, 128, dtype=F32), buf(GROUP - 1, 24, 128, dtype=F32),
        pltpu.SemaphoreType.DMA((14,)), pltpu.SemaphoreType.DMA((2,)),
        pltpu.SemaphoreType.DMA((nchunk, 6)), pltpu.SemaphoreType.DMA((nchunk, 4)),
        pltpu.SemaphoreType.DMA((2 * nrb, 4)), pltpu.SemaphoreType.DMA((2 * nrb, 3)),
        pltpu.SemaphoreType.DMA((2 * GROUP,)), pltpu.SemaphoreType.DMA((2 * GROUP,)),
        pltpu.SemaphoreType.REGULAR((nrb,)),
    ]
    out_shape = [
        jax.ShapeDtypeStruct((rows, width), BF),
        jax.ShapeDtypeStruct((rows, width), BF),
        jax.ShapeDtypeStruct((ff, width), BF),
        jax.ShapeDtypeStruct((width, ff), BF),
        jax.ShapeDtypeStruct((3, width, local), BF),
        jax.ShapeDtypeStruct((local, width), BF),
        jax.ShapeDtypeStruct((width // 64, 128), F32),
        jax.ShapeDtypeStruct((24, 128), F32),
    ]
    macs = rows * width * (6 * ff + 9 * local) + 12 * heads * rows * length * HEAD
    return pl.pallas_call(
        layer_kernel,
        out_shape=out_shape,
        in_specs=[any_spec] * 6 + [vmem] * 9,
        out_specs=[any_spec] * 6 + [vmem] * 2,
        scratch_shapes=scratch,
        compiler_params=pltpu.CompilerParams(
            collective_id=0, has_side_effects=True, vmem_limit_bytes=64 * 2**20 - 2**17
        ),
        cost_estimate=pl.CostEstimate(
            flops=2 * macs, bytes_accessed=40 * 2**20, transcendentals=heads * rows * length
        ),
        name="layer",
    )(x, g, wqkv, wd, w1, w2, seg, gain, lnb, bqkv, db, b1, b2, cos, sin)


def finish_kernel(
    mixed_in, igrad_in, fc2_in, fc1_in, qkv_in, dense_in, norm_ref, bias_ref,
    mixed_out, igrad_out, gain_out, lnb_out, qkv_out, qkvb_out, dense_out, db_out, fc1_out, fc1b_out, fc2_out, b2_out,
    rows16, rows32, qkv16, qkv32, through, pass_sem, load_sem, store_sem,
):
    pieces = []
    step = rows16.shape[1]
    for src, dst in ((dense_in, dense_out), (fc2_in, fc2_out), (fc1_in, fc1_out)):
        for k in range(src.shape[0] // step):
            part, slot = pl.ds(k * step, step), len(pieces)
            pieces.append((src.at[part], dst.at[part], rows16.at[slot], rows32.at[slot]))
    for k in range(3):
        pieces.append((qkv_in.at[k], qkv_out.at[k], qkv16.at[k], qkv32.at[k]))
    loads, stores, passed = [], [], []
    for k, (src, _, low, _) in enumerate(pieces):
        loads.append(pltpu.make_async_copy(src, low, load_sem.at[k]))
        loads[-1].start()
    n = through.shape[1]
    for j, (src, dst) in enumerate(((mixed_in, mixed_out), (igrad_in, igrad_out))):
        for k in range(src.shape[0] // n):
            slot, part = len(passed), pl.ds(k * n, n)
            passed.append((
                pltpu.make_async_copy(src.at[part], through.at[slot], pass_sem.at[0, slot]),
                pltpu.make_async_copy(through.at[slot], dst.at[part], pass_sem.at[1, slot]),
            ))
            passed[-1][0].start()
    for k, (_, dst, low, wide) in enumerate(pieces):
        loads[k].wait()
        step = 32768 // low.shape[1]

        @pl.loop(0, low.shape[0] // step)
        def _(i):
            r = pl.ds(pl.multiple_of(i * step, 16), step)
            wide[r, :] = low[r, :].astype(F32)

        stores.append(pltpu.make_async_copy(wide, dst, store_sem.at[k]))
        stores[-1].start()
    for bring, take in passed:
        bring.wait()
        take.start()
    for k in range(gain_out.shape[1] // 128):
        lanes = slice(k * 128, (k + 1) * 128)
        gain_out[:, lanes] = norm_ref[k:k + 1, :]
        lnb_out[:, lanes] = norm_ref[8 + k:9 + k, :]
        fc1b_out[:, lanes] = bias_ref[k:k + 1, :]
        db_out[:, lanes] = bias_ref[16 + k:17 + k, :]
        b2_out[:, lanes] = bias_ref[16 + k:17 + k, :]
    per = qkvb_out.shape[1] // 128
    for k in range(3 * per):
        qkvb_out[k // per:k // per + 1, k % per * 128:k % per * 128 + 128] = bias_ref[8 + k:9 + k, :]
    for copy in stores + [take for _, take in passed]:
        copy.wait()


def finish(mixed, igrad, fc2, fc1, qkv, dense, norm, bias):
    width, ff, local = fc1.shape[0], fc1.shape[1], dense.shape[0]
    any_spec, vmem = pl.BlockSpec(memory_space=pl.ANY), pl.BlockSpec(memory_space=pltpu.VMEM)

    def wide(array):
        return jax.ShapeDtypeStruct(array.shape, F32)

    line = jax.ShapeDtypeStruct((1, width), F32)
    outs = [
        (mixed, any_spec), (igrad, any_spec), (line, vmem), (line, vmem), (wide(qkv), any_spec),
        (jax.ShapeDtypeStruct((3, local), F32), vmem), (wide(dense), any_spec), (line, vmem),
        (wide(fc1), any_spec), (jax.ShapeDtypeStruct((1, ff), F32), vmem), (wide(fc2), any_spec), (line, vmem),
    ]
    step = 256
    count = (dense.shape[0] + fc2.shape[0] + fc1.shape[0]) // step
    return pl.pallas_call(
        finish_kernel,
        out_shape=[jax.ShapeDtypeStruct(o.shape, o.dtype) for o, _ in outs],
        in_specs=[any_spec] * 6 + [vmem] * 2,
        out_specs=[spec for _, spec in outs],
        scratch_shapes=[
            pltpu.VMEM((count, step, width), BF), pltpu.VMEM((count, step, width), F32),
            pltpu.VMEM(qkv.shape, BF), pltpu.VMEM(qkv.shape, F32),
            pltpu.VMEM((8, mixed.shape[0] // 4, width), BF), pltpu.SemaphoreType.DMA((2, 8)),
            pltpu.SemaphoreType.DMA((count + 3,)), pltpu.SemaphoreType.DMA((count + 3,)),
        ],
        compiler_params=pltpu.CompilerParams(vmem_limit_bytes=56 * 2**20),
        cost_estimate=pl.CostEstimate(flops=0, bytes_accessed=36 * 2**20, transcendentals=0),
        name="finish",
    )(mixed, igrad, fc2, fc1, qkv, dense, norm, bias)


def local_part(
    n_dp, tokens, segment_ids, ln_gain, ln_bias, qkv_weight, qkv_bias, dense_weight, dense_bias,
    fc1_weight, fc1_bias, fc2_weight, fc2_bias, cotangent,
):
    width = tokens.shape[1]
    local = qkv_weight.shape[2]
    cos, sin = rotary_tables(segment_ids.shape[1])
    outs = fused_layer(
        tokens, cotangent, qkv_weight.transpose(1, 0, 2), dense_weight, fc1_weight, fc2_weight,
        segment_ids, ln_gain[None], ln_bias[None], qkv_bias, dense_bias[None],
        fc1_bias[None], fc2_bias[None], cos, sin,
    )
    mixed, igrad, sums = outs[0], outs[1], list(outs[2:])
    if n_dp > GROUP:
        groups = [[k + GROUP * j for j in range(n_dp // GROUP)] for k in range(GROUP)]
        sums = [lax.psum(s, "dp", axis_index_groups=groups) for s in sums]
    done = finish(mixed, igrad, *sums)
    mixed, igrad, gain, lnb, qkv, qkvb, dense, db, fc1, b1, fc2, b2 = done
    return (
        mixed, igrad, gain.reshape(width), lnb.reshape(width), qkv.transpose(1, 0, 2), qkvb, dense,
        db.reshape(width), fc1, b1.reshape(fc1_bias.shape), fc2, b2.reshape(width),
    )


def solution(mesh):
    row, whole = P("dp", None), P()
    weights = (
        whole, whole, P(None, None, "tensor"), P(None, "tensor"), P("tensor", None), whole,
        P(None, "tensor"), P("tensor"), P("tensor", None), whole,
    )
    return jax.shard_map(
        functools.partial(local_part, mesh.shape["dp"]),
        mesh=mesh,
        in_specs=(row, row) + weights + (row,),
        out_specs=(row, row) + weights,
        check_vma=False,
    )
```

```python
import functools
import heapq

import jax
import jax.numpy as jnp
import numpy as np
from jax import lax
from jax.experimental import pallas as pl
from jax.experimental.pallas import tpu as pltpu
from jax.sharding import PartitionSpec as P

HEAD = 64
ROTARY = 32
NORM_EPS = 1e-05
MASKED = -1e30
BASE = 10000.0
BF = jnp.bfloat16
F32 = jnp.float32
MESH = pl.DeviceIdType.MESH
GROUP = 8

ORDER = (
    ("LN", 0), ("FF", 2, 0), ("FF", 1, 0), ("LN", 1), ("LN", 3), ("LN", 2), ("FF", 3, 0), ("FF", 0, 0), ("FF", 0, 1),
    ("FF", 0, 3), ("FF", 0, 2), ("FF", 3, 1), ("FF", 1, 3), ("FF", 2, 3), ("FC2", 0), ("FF", 2, 1), ("FF", 1, 2),
    ("FF", 1, 1), ("FF", 3, 3), ("FF", 2, 2), ("FF", 3, 2), ("FC2", 3), ("FC1", 0), ("PROJ", 0, 0), ("CG", 0, 1),
    ("CG", 0, 0), ("FC1", 1), ("ATT", 0, 0), ("PROJ", 0, 1), ("MIX", 0), ("FC2", 2), ("ATT", 0, 2), ("MIX", 2),
    ("ATT", 0, 3), ("ATT", 0, 1), ("KEY", 0), ("GRAD", 2), ("FC1", 2), ("CG", 1, 1), ("PROJ", 1, 1), ("MIX", 3),
    ("PROJ", 1, 0), ("CG", 1, 0), ("FC1", 3), ("MIX", 1), ("ATT", 1, 0), ("ATT", 1, 1), ("GRAD", 1), ("ATT", 1, 2),
    ("MIX", 6), ("ATT", 1, 3), ("MIX", 4), ("DENSE",), ("MIX", 7), ("KEY", 1), ("QKV", 0), ("QKV", 2), ("GRAD", 3),
    ("QKV", 1), ("GRAD", 7), ("GRAD", 6), ("FC2", 1), ("GRAD", 5), ("GRAD", 4), ("GRAD", 0), ("BIAS",), ("MIX", 5),
)
KINDS = {
    ("FC2", 0): "BA", ("FC2", 1): "AA", ("FC2", 2): "BA", ("FC2", 3): "BA", ("FC1", 0): "AA", ("FC1", 1): "BA",
    ("FC1", 2): "AB", ("FC1", 3): "A", ("QKV", 0): "BA", ("QKV", 1): "AA", ("QKV", 2): "AA", ("DENSE",): "BA",
}


def dot(a, b):
    return lax.dot_general(a, b, (((1,), (0,)), ((), ())), preferred_element_type=F32)


def dot_nt(a, b):
    return lax.dot_general(a, b, (((1,), (1,)), ((), ())), preferred_element_type=F32)


def dot_tn(a, b):
    return lax.dot_general(a, b, (((0,), (0,)), ((), ())), preferred_element_type=F32)


def rotary_table(length):
    half = ROTARY // 2
    frequency = (BASE ** (-(np.arange(half, dtype=np.float32) * 2.0) / ROTARY)).astype(np.float32)
    angles = np.arange(length, dtype=np.float32)[:, None] * frequency[None, :]
    cosine, sine = np.cos(angles), np.sin(angles)
    rest = HEAD - ROTARY
    c = np.concatenate([cosine, cosine, np.ones((length, rest), np.float32)], axis=1)
    s = np.concatenate([-sine, sine, np.zeros((length, rest), np.float32)], axis=1)
    return np.concatenate([c, s], axis=1).astype(np.float32)


def pair_swap(u):
    lane = lax.broadcasted_iota(jnp.int32, u.shape, 1)
    half = ROTARY // 2
    return jnp.where(lane % ROTARY < half, pltpu.roll(u, 128 - half, 1), pltpu.roll(u, half, 1))


class Clock:
    UNIT_KIB = 128
    UNIT_US = 2.85
    CORE_US = 0.4
    LATENCY = 2.8
    MARGIN = 0.5
    STEP_US = 0.12
    ADD_US = 0.03

    def __init__(self):
        self.now = 0.0
        self.queue = []
        self.count = 0
        self.free = {}

    def at(self, when, step):
        heapq.heappush(self.queue, (when, self.count, step))
        self.count += 1

    def arrival(self, link, units):
        start = max(self.now, self.free.get(link, 0.0))
        self.free[link] = start + units * (self.CORE_US if link == "core" else self.UNIT_US)
        return self.free[link] + self.LATENCY + self.MARGIN

    def spend(self, adds=0.0, more=0.0):
        self.now += self.STEP_US + self.ADD_US * adds + more

    def advance(self):
        when, _, step = heapq.heappop(self.queue)
        self.now = max(self.now, when)
        step()

    def due(self):
        while self.queue and self.queue[0][0] <= self.now:
            self.advance()

    def drain(self):
        while self.queue:
            self.advance()


def layer_kernel(
    x_hbm, g_hbm, wqkv_hbm, wd_hbm, w1_hbm, w2_hbm,
    seg_ref, gain_ref, lnb_ref, bqkv_ref, db_ref, b1_ref, b2_ref, rot_ref,
    mixed_hbm, igrad_hbm, fc2_hbm, fc1_hbm, qkv_hbm, dense_hbm, norm_out, bias_out,
    nb, gb, act, dh, wqkv, wd, w1, w2,
    qs, ks, vs, cg, ctx, pg, dkT, dvT, bias, gacc,
    s0, s1, d0, d1,
    pt, t1r, t2r, xs, gA, gQ, gD, rA, rQ, rD,
    norm_send, norm_core, norm_recv, bias_send, bias_recv,
    load_sem, x_sem, dp_send, dp_recv, t_send, t_recv, sm_send, sm_recv, credit,
):
    rows, width = nb.shape
    seqs, length = seg_ref.shape
    local = wd.shape[0]
    ff = w1.shape[1]
    heads = local // HEAD
    QB = 256
    nrb = rows // QB
    HB = QB // 2
    slots = pt.shape[0]

    dp, tensor = lax.axis_index("dp"), lax.axis_index("tensor")
    base = dp - lax.rem(dp, GROUP)
    me = lax.rem(dp, GROUP)
    xx, zz = lax.rem(me, 2), me // 2
    yy, cc = tensor // 2, lax.rem(tensor, 2)
    x_dev = (base + zz * 2 + (1 - xx), tensor)
    pair_dev = (base + (zz + 1 - 2 * lax.rem(zz, 2)) * 2 + xx, tensor)
    mid_dev = (base + (3 - zz) * 2 + xx, tensor)
    y_dev = (dp, (1 - yy) * 2 + cc)
    c_dev = (dp, yy * 2 + (1 - cc))
    side = zz // 2
    inner = (zz == 1) | (zz == 2)
    outer = jnp.logical_not(inner)
    dp_devs = [(base + lax.rem(me + k, GROUP), tensor) for k in range(1, GROUP)]

    barrier = pltpu.get_barrier_semaphore()
    for device in dp_devs + [y_dev, c_dev]:
        pl.semaphore_signal(barrier, inc=1, device_id=device, device_id_type=MESH)

    loads = {}

    def load(name, src, dst):
        loads[name] = pltpu.make_async_copy(src, dst, load_sem.at[len(loads)])
        loads[name].start()

    quarter = rows // 4
    parts = [pl.ds(k * quarter, quarter) for k in range(4)]
    load("x0", x_hbm.at[parts[0]], act.at[parts[0]])
    load("w1", w1_hbm, w1)
    load("w2", w2_hbm, w2)
    load("g0", g_hbm.at[parts[0]], gb.at[parts[0]])
    for k in range(1, 4):
        load(f"x{k}", x_hbm.at[parts[k]], act.at[parts[k]])
        load(f"g{k}", g_hbm.at[parts[k]], gb.at[parts[k]])
    for k in range(3):
        load(f"wqkv{k}", wqkv_hbm.at[k], wqkv.at[:, k * local:(k + 1) * local])
    load("wd", wd_hbm, wd)
    gacc[...] = jnp.zeros_like(gacc)

    clock = Clock()
    cgT = gD.at[:, pl.ds(0, length)]
    last = max(k for k, item in enumerate(ORDER) if item[0] == "ATT")
    late = [item for item in ORDER[last:] if item[0] in ("FC1", "FC2")][-1]
    qT = gA.at[late[1] + (ff // 256 if late[0] == "FC1" else 0), :, pl.ds(0, length)]
    prob_low = [[gQ.at[j, pl.ds(k * QB, QB)] for j in range(3)] for k in range(4)]

    def remote(src, dst, send_sem, recv_sem, device):
        return pltpu.make_async_remote_copy(
            src_ref=src, dst_ref=dst, send_sem=send_sem, recv_sem=recv_sem,
            device_id=device, device_id_type=MESH,
        )

    def span(first, n):
        return pl.ds(pl.multiple_of(first, 16), n)

    def add_rows(dst, a_ref, b_ref):
        n, cols = dst.shape
        step = min(n, 131072 // cols)
        if n % step:
            step = 48

        if n == step:
            dst[...] = a_ref[...] + b_ref[...]
            return

        @pl.loop(0, n // step)
        def _(k):
            r = span(k * step, step)
            dst[r, :] = a_ref[r, :] + b_ref[r, :]

    class PairFirst:
        def __init__(self, k, own, got, out, out_row):
            h = own.shape[0] // 2
            self.h, self.units = h, h * own.shape[1] * 2 / 1024 / clock.UNIT_KIB
            self.xr, self.zi, self.zm = (got.at[pl.ds(j * h, h)] for j in range(3))
            self.keep = own.at[span(xx * h, h)]
            target = out.at[span(out_row + xx * h, h)]
            send, recv = dp_send.at[k], dp_recv.at[k]
            self.c_x = remote(own.at[span((1 - xx) * h, h)], self.xr, send.at[0], recv.at[0], x_dev)
            self.c_in = remote(self.xr, self.zi, send.at[1], recv.at[1], pair_dev)
            self.c_mid = remote(self.zi, self.zm, send.at[2], recv.at[2], mid_dev)
            self.c_out = remote(self.zm, self.zm, send.at[1], recv.at[2], pair_dev)
            self.c_ag = remote(self.zm, target, send.at[3], recv.at[3], x_dev)
            self.c_loc = pltpu.make_async_copy(self.zm, target, send.at[4])

        def start(self):
            self.c_x.start()
            clock.spend()
            clock.at(clock.arrival("x", self.units), self.pair_sum)

        def pair_sum(self):
            self.c_x.wait_recv()
            add_rows(self.xr, self.xr, self.keep)

            @pl.when(outer)
            def _():
                self.c_in.start()

            clock.spend(self.units)
            clock.at(clock.arrival("zin", self.units), self.side_sum)

        def side_sum(self):
            @pl.when(inner)
            def _():
                self.c_in.wait_recv()
                add_rows(self.zi, self.zi, self.xr)
                self.c_mid.start()

            clock.spend(self.units)
            clock.at(clock.arrival("zmid", self.units), self.line_sum)

        def line_sum(self):
            @pl.when(inner)
            def _():
                self.c_mid.wait_recv()
                self.c_mid.wait_send()
                add_rows(self.zm, self.zm, self.zi)
                self.c_out.start()
                self.c_ag.start()
                self.c_loc.start()

            clock.spend(self.units)
            clock.at(clock.arrival("zout", self.units), self.outer_end)

        def outer_end(self):
            @pl.when(outer)
            def _():
                self.c_mid.wait_recv()
                self.c_ag.start()
                self.c_loc.start()

            clock.spend()
            clock.arrival("x", self.units)

        def finish(self):
            self.c_x.wait_send()
            self.c_in.wait_send()
            self.c_ag.wait()
            self.c_loc.wait()

    class LineFirst:
        def __init__(self, k, own, got, out, out_row):
            n = own.shape[0]
            b = n // 4
            self.b, self.units = b, b * own.shape[1] * 2 / 1024 / clock.UNIT_KIB
            self.r1, self.r2, self.xb = got.at[pl.ds(0, 3 * b)], got.at[pl.ds(3 * b, 2 * b)], got.at[pl.ds(5 * b, b)]
            rest = own.at[span((1 - side) * b, 3 * b)]
            self.mine = own.at[span(zz * b, b)]
            self.far = own.at[span((1 - side) * 2 * b, 2 * b)]
            near = own.at[span(side * 2 * b, 2 * b)]
            self.outers = own.at[span(side * 3 * b, b)]
            self.r1_far = self.r1.at[span((1 - side) * b, 2 * b)]
            self.r1_mine = self.r1.at[span(side * 2 * b, b)]
            self.r2_mine = self.r2.at[span((1 - side) * b, b)]
            self.r2_outer = self.r2.at[span(side * b, b)]
            r1_first = self.r1.at[pl.ds(0, b)]
            self.r1_first = r1_first
            send, recv = dp_send.at[k], dp_recv.at[k]
            self.c_1 = remote(rest, self.r1, send.at[0], recv.at[0], pair_dev)
            self.c_2 = remote(self.r1_far, self.r2, send.at[0], recv.at[1], mid_dev)
            self.c_3 = remote(self.r2_outer, r1_first, send.at[1], recv.at[0], pair_dev)
            self.c_x = remote(self.mine, self.xb, send.at[2], recv.at[2], x_dev)
            self.c_5 = remote(self.mine, self.mine, send.at[1], recv.at[3], pair_dev)
            self.c_5r = remote(self.outers, self.outers, send.at[1], recv.at[3], pair_dev)
            self.c_6 = remote(near, near, send.at[3], recv.at[1], mid_dev)
            self.c_6r = remote(self.far, self.far, send.at[3], recv.at[1], mid_dev)
            self.c_7 = remote(rest, rest, send.at[4], recv.at[3], pair_dev)
            self.c_loc = pltpu.make_async_copy(own, out.at[span(out_row, n)], send.at[5])

        def start(self):
            @pl.when(outer)
            def _():
                self.c_1.start()

            clock.spend(2 * self.units)
            clock.at(clock.arrival("zin", 3 * self.units), self.side_sum)

        def side_sum(self):
            @pl.when(inner)
            def _():
                self.c_1.wait_recv()
                add_rows(self.r1_far, self.r1_far, self.far)
                self.c_2.start()
                add_rows(self.r1_mine, self.r1_mine, self.mine)

            clock.spend(2 * self.units)
            clock.at(clock.arrival("zmid", 2 * self.units), self.line_sum)

        def line_sum(self):
            @pl.when(inner)
            def _():
                self.c_2.wait_recv()
                add_rows(self.r2_outer, self.r2_outer, self.outers)
                self.c_3.start()
                add_rows(self.mine, self.r1_mine, self.r2_mine)
                self.c_x.start()

            clock.spend(2 * self.units)
            clock.at(clock.arrival("zout", self.units), self.outer_sum)

        def outer_sum(self):
            @pl.when(outer)
            def _():
                self.c_3.wait_recv()
                add_rows(self.mine, self.mine, self.r1_first)
                self.c_x.start()

            clock.spend(2 * self.units)
            clock.at(clock.arrival("x", self.units), self.pair_sum)

        def pair_sum(self):
            self.c_x.wait()
            add_rows(self.mine, self.mine, self.xb)

            @pl.when(outer)
            def _():
                self.c_1.wait_send()
                self.c_5.start()

            clock.spend(2 * self.units)
            clock.at(clock.arrival("zin", self.units), self.side_gather)

        def side_gather(self):
            @pl.when(inner)
            def _():
                self.c_5r.wait_recv()
                self.c_6.start()

            clock.spend(2 * self.units)
            clock.at(clock.arrival("zmid", 2 * self.units), self.line_gather)

        def line_gather(self):
            @pl.when(inner)
            def _():
                self.c_6r.wait_recv()
                self.c_7.start()
                self.c_loc.start()

            clock.spend(2 * self.units)
            clock.at(clock.arrival("zout", 3 * self.units), self.outer_end)

        def outer_end(self):
            @pl.when(outer)
            def _():
                self.c_7.wait_recv()
                self.c_loc.start()

        def finish(self):
            @pl.when(outer)
            def _():
                self.c_5.wait_send()

            @pl.when(inner)
            def _():
                self.c_2.wait_send()
                self.c_3.wait_send()
                self.c_6.wait_send()
                self.c_7.wait_send()

            self.c_loc.wait()

    chunks = []

    kind_of = {"A": PairFirst, "B": LineFirst}

    waited = []

    def entered():
        if not waited:
            pl.semaphore_wait(barrier, len(dp_devs) + 2)
            waited.append(True)

    def new_chunk(own, got, out, out_row, kinds):
        entered()
        n, m = own.shape[0] // len(kinds), got.shape[0] // len(kinds)
        for k, kind in enumerate(kinds):
            part = own.at[pl.ds(k * n, n)]
            chunk = kind_of[kind](len(chunks), part, got.at[pl.ds(k * m, m)], out, out_row + k * n)
            chunks.append(chunk)
            chunk.start()

    y_order = []
    mine = span(cc * HB, HB)
    other = span((1 - cc) * HB, HB)

    def fetch(seq):
        if seq < len(y_order):
            rb = y_order[seq][1]
            src = x_hbm.at[span(rb * QB + cc * HB, HB)]
            pltpu.make_async_copy(src, xs, x_sem.at[0]).start()

    def row_stats(x):
        mu = jnp.mean(x, axis=1, keepdims=True)
        cent = x - mu
        rstd = lax.rsqrt(jnp.mean(cent * cent, axis=1, keepdims=True) + NORM_EPS)
        return cent * rstd, rstd

    class RowSum:
        def __init__(self, phase, rb):
            self.phase, self.rb, self.done = phase, rb, False
            self.seq = k = y_order.index((phase, rb))
            self.slot = slot = k % slots
            out = igrad_hbm if phase else mixed_hbm
            target = out.at[span(rb * QB + cc * HB, HB)]
            self.own = own = pt.at[slot, mine]
            self.units = HB * width * 2 / 1024 / clock.UNIT_KIB
            send, recv = t_send.at[k], t_recv.at[k]
            self.c_core = remote(pt.at[slot, other], t1r.at[slot], send.at[0], recv.at[0], c_dev)
            self.c_y = remote(own, t2r.at[slot], send.at[1], recv.at[1], y_dev)
            self.c_fin = remote(t2r.at[slot], target, send.at[2], recv.at[2], c_dev)
            self.c_loc = pltpu.make_async_copy(t2r.at[slot], target, send.at[3])

        def start(self):
            if self.seq >= slots:
                row_sums[y_order[self.seq - slots]].c_fin.wait_recv()
            self.c_core.start()
            clock.spend()
            clock.at(clock.arrival("core", self.units), self.chip_sum)

        def chip_sum(self):
            self.c_core.wait_recv()
            add_rows(self.own, self.own, t1r.at[self.slot])
            if self.seq >= slots:
                pl.semaphore_wait(credit.at[self.slot], 1)
            self.c_y.start()
            clock.spend(self.units)
            clock.at(clock.arrival("y", self.units), self.whole_sum)

        def whole_sum(self):
            rb = self.rb
            pltpu.make_async_copy(x_hbm.at[pl.ds(0, HB)], xs, x_sem.at[0]).wait()
            self.c_y.wait_recv()
            step = 16
            own, arrived = self.own, t2r.at[self.slot]
            gsum, bsum = gacc[0:8, :], gacc[8:16, :]
            for j in range(HB // step):
                first = j * step
                r = pl.ds(first, step)
                x = xs[r, :].astype(F32)
                total = own[r, :].astype(F32) + arrived[r, :].astype(F32)
                if self.phase == 0:
                    arrived[r, :] = (x + total + (db_ref[...] + b2_ref[...])).astype(BF)
                else:
                    xhat, rstd = row_stats(x)
                    gsum += jnp.sum((total * xhat).reshape(step // 8, 8, width), axis=0)
                    bsum += jnp.sum(total.reshape(step // 8, 8, width), axis=0)
                    e = total * gain_ref[...]
                    m1 = jnp.mean(e, axis=1, keepdims=True)
                    m2 = jnp.mean(e * xhat, axis=1, keepdims=True)
                    gr = span(rb * QB + cc * HB + first, step)
                    grad = gb[gr, :].astype(F32) + rstd * (e - m1 - xhat * m2)
                    arrived[r, :] = grad.astype(BF)
            if self.phase:
                gacc[0:8, :], gacc[8:16, :] = gsum, bsum
            fetch(self.seq + 1)
            self.c_fin.start()
            self.c_loc.start()
            clock.spend(0, 0.5 if self.phase else 0.3)
            if self.seq + slots < len(y_order):
                clock.at(clock.now + 4.0, self.give_back)
            if self.phase and all(phase == 0 for phase, _ in y_order[self.seq + 1:]):
                clock.at(clock.now, norm_sums)

        def give_back(self):
            clock.spend()
            self.c_fin.wait_send()
            self.c_loc.wait()
            self.c_core.wait_send()
            self.c_y.wait_send()
            pl.semaphore_signal(credit.at[self.slot], inc=1, device_id=y_dev, device_id_type=MESH)
            self.done = True

        def finish(self):
            if not self.done:
                self.c_core.wait_send()
                self.c_y.wait_send()
                self.c_fin.wait()
                self.c_loc.wait()

    row_sums = {}

    def new_rows(phase, rb):
        entered()
        row_sums[(phase, rb)] = RowSum(phase, rb)
        row_sums[(phase, rb)].start()

    def free_slot(phase, rb):
        seq = y_order.index((phase, rb))
        while seq >= slots and not row_sums[y_order[seq - slots]].done:
            clock.advance()
        return seq % slots

    small = []

    def fold(dst, first, line):
        for k in range(line.shape[1] // 128):
            dst[first + k:first + k + 1, :] = line[:, k * 128:(k + 1) * 128]

    def send_small(src, slots, first_sem):
        for k, device in enumerate(dp_devs):
            sem = first_sem + k
            copy = remote(src, slots.at[k], sm_send.at[sem], sm_recv.at[sem], device)
            copy.start()
            small.append(copy)

    def sum_small(src, slots):
        total = jnp.zeros(src.shape, F32)
        for place in range(GROUP):
            behind = lax.rem(me - place + GROUP, GROUP)
            there = slots[jnp.maximum(behind - 1, 0)]
            total = total + jnp.where(behind == 0, src[...], there)
        return total

    def bias_sums():
        ones = jnp.ones((16, rows), BF)
        bias_send[...] = jnp.zeros_like(bias_send)
        for k, array in enumerate((dh, pg, gb)):
            fold(bias_send, 8 * k, dot(ones, array[...])[0:1, :])
        send_small(bias_send, bias_recv, 1)

    def norm_sums():
        for k in range(2):
            fold(norm_send, 8 * k, jnp.sum(gacc[8 * k:8 * k + 8, :], axis=0, keepdims=True))
        swap = remote(norm_send, norm_core, sm_send.at[0], sm_recv.at[0], c_dev)
        swap.start()
        swap.wait()
        norm_send[...] = norm_send[...] + norm_core[...]
        send_small(norm_send, norm_recv, GROUP)

    def small_finish():
        for copy in small:
            copy.wait()
        norm_out[...] = sum_small(norm_send, norm_recv)
        bias_out[...] = sum_small(bias_send, bias_recv)

    def wait_load(*names):
        for name in names:
            if name in loads:
                loads.pop(name).wait()

    def norm_forward(k):
        step = 16
        wait_load(f"x{k}")
        for j in range(quarter // step):
            r = slice(k * quarter + j * step, k * quarter + (j + 1) * step)
            xhat, _ = row_stats(act[r, :].astype(F32))
            nb[r, :] = (xhat * gain_ref[...] + lnb_ref[...]).astype(BF)

    def ff_products(j, q, slot):
        wait_load("w1", "w2", f"g{q}")
        cols, r = slice(j * 256, (j + 1) * 256), slice(q * quarter, (q + 1) * quarter)
        h = dot(nb[r, :], w1[:, cols])
        up = dot_nt(gb[r, :], w2[cols, :])
        for k in range(quarter // 256):
            (s0, s1)[slot][:, k * 256:(k + 1) * 256] = h[k * 256:(k + 1) * 256]
            (d0, d1)[slot][:, k * 256:(k + 1) * 256] = up[k * 256:(k + 1) * 256]

    def ff_gelu(j, q, slot):
        cols = slice(j * 256, (j + 1) * 256)
        step = 32
        k0 = 0.7978845608028654
        for t in range(quarter // step):
            at = slice(t * step % 256, t * step % 256 + step)
            lane = slice(t * step // 256 * 256, t * step // 256 * 256 + 256)
            r = slice(q * quarter + t * step, q * quarter + (t + 1) * step)
            h = (s0, s1)[slot][at, lane] + b1_ref[:, cols]
            up = (d0, d1)[slot][at, lane]
            h2 = h * h
            th = jnp.tanh(k0 * h * (1.0 + 0.044715 * h2))
            half = 0.5 * (1.0 + th)
            act[r, cols] = (h * half).astype(BF)
            slope = half + 0.5 * h * (1.0 - th * th) * (k0 * (1.0 + 3 * 0.044715 * h2))
            hg = (up * slope).astype(BF)
            dh[r, cols] = hg

    ahead = {"slot": 0, "ready": False}

    def feed_forward(j, q, following=None):
        slot = ahead["slot"]
        if not ahead["ready"]:
            ff_products(j, q, slot)
        if following:
            ff_products(*following, 1 - slot)
        ahead["slot"], ahead["ready"] = 1 - slot, bool(following)
        ff_gelu(j, q, slot)

    nf = ff // 256

    def fc2_chunk(j, kind):
        wait_load("g0", "g1", "g2", "g3")
        gA[j] = dot_tn(act[:, j * 256:(j + 1) * 256], gb[...]).astype(BF)
        new_chunk(gA.at[j], rA.at[j], fc2_hbm, j * 256, kind)

    def fc1_chunk(j, kind):
        k = nf + j
        gA[k] = dot_tn(nb[:, j * 256:(j + 1) * 256], dh[...]).astype(BF)
        new_chunk(gA.at[k], rA.at[k], fc1_hbm, j * 256, kind)

    def qkv_chunk(j, kind):
        for k in range(2):
            at = slice(k * width // 2, (k + 1) * width // 2)
            gQ[j, at, :] = dot_tn(nb[:, at], pg[:, j * local:(j + 1) * local]).astype(BF)
        new_chunk(gQ.at[j], rQ.at[j], qkv_hbm.at[j], 0, kind)

    def dense_chunk(kind):
        gD[...] = dot_tn(ctx[...], gb[...]).astype(BF)
        new_chunk(gD, rD, dense_hbm, 0, kind)

    def rotary(r):
        both = rot_ref[r, :]
        turned = pltpu.roll(both, HEAD, 1)
        low = lax.broadcasted_iota(jnp.int32, both.shape, 1) < HEAD
        return jnp.where(low, both, turned), jnp.where(low, turned, both)

    def project(s, half):
        wait_load("wqkv0", "wqkv1", "wqkv2")
        for i in range(half * length // 512, (half + 1) * length // 512):
            r = slice(i * 256, (i + 1) * 256)
            src = slice(s * length + i * 256, s * length + (i + 1) * 256)
            c, sn = rotary(r)
            whole = dot(nb[src, :], wqkv[...])
            for part in range(3):
                y = whole[:, part * local:(part + 1) * local] + bqkv_ref[part:part + 1, :]
                for pr in range(heads // 2):
                    lanes = slice(pr * 128, (pr + 1) * 128)
                    u = y[:, lanes]
                    if part < 2:
                        u = u * c + pair_swap(u) * sn
                    if part == 0:
                        u = u * (HEAD ** -0.5)
                        qT[lanes, r] = u.T.astype(BF)
                    (qs, ks, vs)[part][r, lanes] = u.astype(BF)

    def context_grad(s, half):
        wait_load("wd", f"g{2 * s + half}")
        r = slice(half * length // 2, (half + 1) * length // 2)
        u = dot_nt(gb[s * length + half * length // 2:s * length + (half + 1) * length // 2, :], wd[...])
        cg[r, :] = u.astype(BF)
        cgT[:, r] = u.T.astype(BF)

    touched = set()

    def attend(s, i):
        blocks = length // QB
        lo = max(0, i - blocks // 2)
        n = (i + 1 - lo) * QB
        qrows = slice(i * QB, (i + 1) * QB)
        keys = slice(lo * QB, (i + 1) * QB)
        at_rows = slice(s * length + i * QB, s * length + (i + 1) * QB)
        seg = seg_ref[s:s + 1, :].astype(F32)
        qseg = jnp.broadcast_to(seg[:, qrows], (128, QB)).T
        for t in range(n // 128):
            at = lo * QB + t * 128
            kseg = jnp.broadcast_to(seg[:, at:at + 128], (QB, 128))
            qpos = i * QB + lax.broadcasted_iota(jnp.int32, (QB, 128), 0)
            kpos = at + lax.broadcasted_iota(jnp.int32, (QB, 128), 1)
            ok = (kpos <= qpos) & (kseg == qseg)
            bias[:, t * 128:(t + 1) * 128] = jnp.where(ok, 0.0, MASKED)
        low = lax.broadcasted_iota(jnp.int32, (QB, 128), 1) < HEAD
        zero = jnp.zeros((), BF)
        c, sn = rotary(qrows)

        def head_of(u, h):
            return jnp.where(low, u, zero) if h % 2 == 0 else jnp.where(low, zero, u)

        def scores(h):
            lanes = slice(h // 2 * 128, h // 2 * 128 + 128)
            (s0, s1)[h % 2][:, :n] = dot_nt(head_of(qs[qrows, lanes], h), ks[keys, lanes])
            (d0, d1)[h % 2][:, :n] = dot_nt(head_of(cg[qrows, lanes], h), vs[keys, lanes])

        def soft(h):
            step = 16
            sc_ref, dp_ref = (s0, s1)[h % 2], (d0, d1)[h % 2]

            def put(dst, r, first, value):
                for j in range(first // HB, first // HB + value.shape[1] // HB):
                    dst[j // 2][r, j % 2 * HB:(j % 2 + 1) * HB] = value[:, j * HB - first:(j + 1) * HB - first]

            for t in range(QB // step):
                r = slice(t * step, (t + 1) * step)
                top = i * QB + t * step // HB * HB
                first, last = max(0, top - length // 2) - lo * QB, top + HB - lo * QB
                first = max(0, first)
                if h < 2:
                    for gap, wide in ((0, first), (last, n - last)):
                        if wide:
                            for dst in (prob_low[h % 2], prob_low[2 + h % 2]):
                                put(dst, r, gap, jnp.zeros((step, wide), BF))
                sc = sc_ref[r, first:last] + bias[r, first:last]
                e = jnp.exp(sc - jnp.max(sc, axis=1, keepdims=True))
                p = e * (1.0 / jnp.sum(e, axis=1, keepdims=True))
                put(prob_low[h % 2], r, first, p.astype(BF))
                pd = p * dp_ref[r, first:last]
                delta = jnp.sum(pd, axis=1, keepdims=True)
                put(prob_low[2 + h % 2], r, first, (pd - p * delta).astype(BF))

        def products(h, kept):
            lanes = slice(h // 2 * 128, h // 2 * 128 + 128)
            hr = slice(h * HEAD, (h + 1) * HEAD)
            p, e = (jnp.concatenate([prob_low[k][j][...] for j in range(n // QB)], axis=1) for k in (h % 2, 2 + h % 2))
            kept.append((dot(p, vs[keys, lanes]), dot(e, ks[keys, lanes])))
            for total, new in ((dvT, dot(cgT[hr, qrows], p)), (dkT, dot(qT[hr, qrows], e))):
                for j in range(n // QB):
                    at = slice((lo + j) * QB, (lo + j + 1) * QB)
                    part = new[:, j * QB:(j + 1) * QB]
                    total[hr, at] = total[hr, at] + part if (s, lo + j) in touched else part
            if h % 2:
                (o_a, q_a), (o_b, q_b) = kept
                kept.clear()
                ctx[at_rows, lanes] = jnp.where(low, o_a, o_b).astype(BF)
                u = jnp.where(low, q_a, q_b) * (HEAD ** -0.5)
                u = u * c - pair_swap(u) * sn
                pg[at_rows, lanes] = u.astype(BF)

        kept = []
        scores(0)
        for h in range(heads):
            if h + 1 < heads:
                scores(h + 1)
            soft(h)
            products(h, kept)
        touched.update((s, lo + j) for j in range(n // QB))

    def key_grads(s):
        for i in range(length // 256):
            r = slice(i * 256, (i + 1) * 256)
            dst = slice(s * length + i * 256, s * length + (i + 1) * 256)
            c, sn = rotary(r)
            for pr in range(heads // 2):
                u = dkT[pr * 128:(pr + 1) * 128, r].T
                u = u * c - pair_swap(u) * sn
                pg[dst, local + pr * 128:local + (pr + 1) * 128] = u.astype(BF)
                u = dvT[pr * 128:(pr + 1) * 128, r].T
                pg[dst, 2 * local + pr * 128:2 * local + (pr + 1) * 128] = u.astype(BF)


    def mix_rows(rb):
        r = slice(rb * QB, (rb + 1) * QB)
        pt[free_slot(0, rb)] = (dot(act[r, :], w2[...]) + dot(ctx[r, :], wd[...])).astype(BF)
        new_rows(0, rb)

    def grad_rows(rb):
        r = slice(rb * QB, (rb + 1) * QB)
        pt[free_slot(1, rb)] = (dot_nt(dh[r, :], w1[...]) + dot_nt(pg[r, :], wqkv[...])).astype(BF)
        new_rows(1, rb)

    pieces = {
        "LN": (0.79, norm_forward), "FF": (0.63, feed_forward),
        "FC2": (1.31, fc2_chunk), "FC1": (1.31, fc1_chunk), "QKV": (1.26, qkv_chunk), "DENSE": (1.26, dense_chunk),
        "PROJ": (1.1, project), "CG": (0.42, context_grad), "ATT": (0.89, attend), "KEY": (1.37, key_grads),
        "MIX": (0.74, mix_rows), "GRAD": (1.02, grad_rows), "BIAS": (1.26, bias_sums),
    }
    y_order += [(0 if item[0] == "MIX" else 1, item[1]) for item in ORDER if item[0] in ("MIX", "GRAD")]
    fetch(0)
    clock.now = 4.0
    run = 0
    for k, item in enumerate(ORDER):
        run = run + 1 if k and item[0] == ORDER[k - 1][0] == "FF" else 0
        if run % 6 == 0:
            clock.due()
        name, args = item[0], list(item[1:])
        cost, fn = pieces[name]
        if name in ("MIX", "GRAD"):
            free_slot(0 if name == "MIX" else 1, args[0])
        if name == "ATT":
            cost = cost * min(args[1] + 1, 3) + 0.26
        if name == "FF":
            chained = k + 1 < len(ORDER) and ORDER[k + 1][0] == "FF"
            cost += 0.0 if ahead["ready"] else 0.37
            args.append(ORDER[k + 1][1:] if chained else None)
        if name in ("FC2", "FC1", "QKV", "DENSE"):
            args.append(KINDS[item])
        clock.now += cost
        fn(*args)
    clock.drain()
    for chunk in chunks:
        chunk.finish()
    for item in row_sums.values():
        item.finish()
    small_finish()


def fused_layer(x, g, wqkv, wd, w1, w2, seg, gain, lnb, bqkv, db, b1, b2, rot):
    rows, width = x.shape
    local, ff = wd.shape[0], w1.shape[1]
    length = seg.shape[1]
    heads = local // HEAD
    nf, nrb = ff // 256, rows // 256
    slots = min(7, 2 * nrb)
    nchunk = sum(len(kinds) for kinds in KINDS.values())
    any_spec, vmem = pl.BlockSpec(memory_space=pl.ANY), pl.BlockSpec(memory_space=pltpu.VMEM)

    def buf(*shape, dtype=BF):
        return pltpu.VMEM(shape, dtype)

    band = length // 2 + 256
    scratch = [
        buf(rows, width), buf(rows, width), buf(rows, ff), buf(rows, ff),
        buf(width, 3 * local), buf(local, width), buf(width, ff), buf(ff, width),
        buf(length, local), buf(length, local), buf(length, local),
        buf(length, local), buf(rows, local), buf(rows, 3 * local),
        buf(local, length, dtype=F32), buf(local, length, dtype=F32),
        buf(256, band, dtype=F32), buf(16, width, dtype=F32),
    ]
    scratch += [buf(256, band, dtype=F32)] * 4
    scratch += [
        buf(slots, 256, width), buf(slots, 128, width), buf(slots, 128, width), buf(128, width),
        buf(2 * nf, 256, width), buf(3, width, local), buf(local, width),
        buf(2 * nf, 384, width), buf(3, width * 3 // 2, local), buf(local * 3 // 2, width),
        buf(width // 64, 128, dtype=F32), buf(width // 64, 128, dtype=F32),
        buf(GROUP - 1, width // 64, 128, dtype=F32),
        buf(24, 128, dtype=F32), buf(GROUP - 1, 24, 128, dtype=F32),
        pltpu.SemaphoreType.DMA((14,)), pltpu.SemaphoreType.DMA((1,)),
        pltpu.SemaphoreType.DMA((nchunk, 6)), pltpu.SemaphoreType.DMA((nchunk, 4)),
        pltpu.SemaphoreType.DMA((2 * nrb, 4)), pltpu.SemaphoreType.DMA((2 * nrb, 3)),
        pltpu.SemaphoreType.DMA((2 * GROUP,)), pltpu.SemaphoreType.DMA((2 * GROUP,)),
        pltpu.SemaphoreType.REGULAR((slots,)),
    ]
    out_shape = [
        jax.ShapeDtypeStruct((rows, width), BF),
        jax.ShapeDtypeStruct((rows, width), BF),
        jax.ShapeDtypeStruct((ff, width), BF),
        jax.ShapeDtypeStruct((width, ff), BF),
        jax.ShapeDtypeStruct((3, width, local), BF),
        jax.ShapeDtypeStruct((local, width), BF),
        jax.ShapeDtypeStruct((width // 64, 128), F32),
        jax.ShapeDtypeStruct((24, 128), F32),
    ]
    macs = rows * width * (6 * ff + 9 * local) + 12 * heads * rows * length * HEAD
    return pl.pallas_call(
        layer_kernel,
        out_shape=out_shape,
        in_specs=[any_spec] * 6 + [vmem] * 8,
        out_specs=[any_spec] * 6 + [vmem] * 2,
        scratch_shapes=scratch,
        compiler_params=pltpu.CompilerParams(
            collective_id=0, has_side_effects=True, vmem_limit_bytes=64 * 2**20 - 2**17
        ),
        cost_estimate=pl.CostEstimate(
            flops=2 * macs, bytes_accessed=40 * 2**20, transcendentals=heads * rows * length
        ),
        name="layer",
    )(x, g, wqkv, wd, w1, w2, seg, gain, lnb, bqkv, db, b1, b2, rot)


def finish_kernel(
    mixed_in, igrad_in, fc2_in, fc1_in, qkv_in, dense_in, norm_ref, bias_ref,
    mixed_out, igrad_out, gain_out, lnb_out, qkv_out, qkvb_out, dense_out, db_out, fc1_out, fc1b_out, fc2_out, b2_out,
    rows16, rows32, qkv16, qkv32, through, pass_sem, load_sem, store_sem,
):
    pieces = []
    step = rows16.shape[1]
    for src, dst in ((dense_in, dense_out), (fc2_in, fc2_out), (fc1_in, fc1_out)):
        for k in range(src.shape[0] // step):
            part, slot = pl.ds(k * step, step), len(pieces)
            pieces.append((src.at[part], dst.at[part], rows16.at[slot], rows32.at[slot]))
    for k in range(3):
        pieces.append((qkv_in.at[k], qkv_out.at[k], qkv16.at[k], qkv32.at[k]))
    loads, stores, passed = [], [], []
    for k, (src, _, low, _) in enumerate(pieces):
        loads.append(pltpu.make_async_copy(src, low, load_sem.at[k]))
        loads[-1].start()
    n = through.shape[1]
    for j, (src, dst) in enumerate(((mixed_in, mixed_out), (igrad_in, igrad_out))):
        for k in range(src.shape[0] // n):
            slot, part = len(passed), pl.ds(k * n, n)
            passed.append((
                pltpu.make_async_copy(src.at[part], through.at[slot], pass_sem.at[0, slot]),
                pltpu.make_async_copy(through.at[slot], dst.at[part], pass_sem.at[1, slot]),
            ))
            passed[-1][0].start()
    for k, (_, dst, low, wide) in enumerate(pieces):
        loads[k].wait()
        step = 32768 // low.shape[1]

        @pl.loop(0, low.shape[0] // step)
        def _(i):
            r = pl.ds(pl.multiple_of(i * step, 16), step)
            wide[r, :] = low[r, :].astype(F32)

        stores.append(pltpu.make_async_copy(wide, dst, store_sem.at[k]))
        stores[-1].start()
    for bring, take in passed:
        bring.wait()
        take.start()
    for k in range(gain_out.shape[1] // 128):
        lanes = slice(k * 128, (k + 1) * 128)
        gain_out[:, lanes] = norm_ref[k:k + 1, :]
        lnb_out[:, lanes] = norm_ref[8 + k:9 + k, :]
        fc1b_out[:, lanes] = bias_ref[k:k + 1, :]
        db_out[:, lanes] = bias_ref[16 + k:17 + k, :]
        b2_out[:, lanes] = bias_ref[16 + k:17 + k, :]
    per = qkvb_out.shape[1] // 128
    for k in range(3 * per):
        qkvb_out[k // per:k // per + 1, k % per * 128:k % per * 128 + 128] = bias_ref[8 + k:9 + k, :]
    for copy in stores + [take for _, take in passed]:
        copy.wait()


def finish(mixed, igrad, fc2, fc1, qkv, dense, norm, bias):
    width, ff, local = fc1.shape[0], fc1.shape[1], dense.shape[0]
    any_spec, vmem = pl.BlockSpec(memory_space=pl.ANY), pl.BlockSpec(memory_space=pltpu.VMEM)

    def wide(array):
        return jax.ShapeDtypeStruct(array.shape, F32)

    line = jax.ShapeDtypeStruct((1, width), F32)
    outs = [
        (mixed, any_spec), (igrad, any_spec), (line, vmem), (line, vmem), (wide(qkv), any_spec),
        (jax.ShapeDtypeStruct((3, local), F32), vmem), (wide(dense), any_spec), (line, vmem),
        (wide(fc1), any_spec), (jax.ShapeDtypeStruct((1, ff), F32), vmem), (wide(fc2), any_spec), (line, vmem),
    ]
    step = 256
    count = (dense.shape[0] + fc2.shape[0] + fc1.shape[0]) // step
    return pl.pallas_call(
        finish_kernel,
        out_shape=[jax.ShapeDtypeStruct(o.shape, o.dtype) for o, _ in outs],
        in_specs=[any_spec] * 6 + [vmem] * 2,
        out_specs=[spec for _, spec in outs],
        scratch_shapes=[
            pltpu.VMEM((count, step, width), BF), pltpu.VMEM((count, step, width), F32),
            pltpu.VMEM(qkv.shape, BF), pltpu.VMEM(qkv.shape, F32),
            pltpu.VMEM((4, mixed.shape[0] // 2, width), BF), pltpu.SemaphoreType.DMA((2, 4)),
            pltpu.SemaphoreType.DMA((count + 3,)), pltpu.SemaphoreType.DMA((count + 3,)),
        ],
        compiler_params=pltpu.CompilerParams(vmem_limit_bytes=56 * 2**20),
        cost_estimate=pl.CostEstimate(flops=0, bytes_accessed=36 * 2**20, transcendentals=0),
        name="finish",
    )(mixed, igrad, fc2, fc1, qkv, dense, norm, bias)


def local_part(
    n_dp, tokens, segment_ids, ln_gain, ln_bias, qkv_weight, qkv_bias, dense_weight, dense_bias,
    fc1_weight, fc1_bias, fc2_weight, fc2_bias, cotangent,
):
    width = tokens.shape[1]
    local = qkv_weight.shape[2]
    rot = rotary_table(segment_ids.shape[1])
    outs = fused_layer(
        tokens, cotangent, qkv_weight.transpose(1, 0, 2), dense_weight, fc1_weight, fc2_weight,
        segment_ids, ln_gain[None], ln_bias[None], qkv_bias, dense_bias[None],
        fc1_bias[None], fc2_bias[None], rot,
    )
    mixed, igrad, sums = outs[0], outs[1], list(outs[2:])
    if n_dp > GROUP:
        groups = [[k + GROUP * j for j in range(n_dp // GROUP)] for k in range(GROUP)]
        sums = [lax.psum(s, "dp", axis_index_groups=groups) for s in sums]
    done = finish(mixed, igrad, *sums)
    mixed, igrad, gain, lnb, qkv, qkvb, dense, db, fc1, b1, fc2, b2 = done
    return (
        mixed, igrad, gain.reshape(width), lnb.reshape(width), qkv.transpose(1, 0, 2), qkvb, dense,
        db.reshape(width), fc1, b1.reshape(fc1_bias.shape), fc2, b2.reshape(width),
    )


def solution(mesh):
    row, whole = P("dp", None), P()
    weights = (
        whole, whole, P(None, None, "tensor"), P(None, "tensor"), P("tensor", None), whole,
        P(None, "tensor"), P("tensor"), P("tensor", None), whole,
    )
    return jax.shard_map(
        functools.partial(local_part, mesh.shape["dp"]),
        mesh=mesh,
        in_specs=(row, row) + weights + (row,),
        out_specs=(row, row) + weights,
        check_vma=False,
    )
```
